256 devices in a mesh: sub: 32 (over x, z), load: 8 (over y, core).
Axes of the slice: x: 4, y: 4, z: 8, core: 2. Of those that a mesh axis runs over, the one named last changes fastest.
Arguments:
- dual_ops: bfloat16 [256, 1024, 1024], P(('sub', 'load')), may hold values from -0.1875 to 0.1875
- dual_rhs: float32 [256, 1024, 128], P(('sub', 'load')), may hold values from -6 to 6
- partner: int32 [256, 1024], P(('sub', 'load')), may hold values from 0 to 3071, as said below
- coarse_basis: bfloat16 [256, 12, 1024], P(('sub', 'load')), may hold values from -0.1875 to 0.1875
- coarse_inverse: float32 [3072, 3072], P(('sub', 'load')), as said below
- damping: float32 [128], replicated, may hold values from 0.05 to 0.5
- recovery: bfloat16 [256, 1536, 1024], P(('sub', 'load')), may hold values from -0.1875 to 0.1875
- base_disp: bfloat16 [256, 1536, 128], P(('sub', 'load')), may hold values from -6 to 6
- adjoint: bfloat16 [256, 1536, 128], P(('sub', 'load')), may hold values from -6 to 6
- elem_voxel: int32 [256, 128], P(('sub', 'load')), may hold values from 0 to 32767
- fibre_class: int32 [256, 1024], P('sub', 'load'), may hold values from 0 to 3
Outputs:
- multipliers: float32 [256, 1024, 128], P(('sub', 'load'))
- gradient_field: float32 [256, 1024], P('sub', 'load')
The draws below stay inside these ranges and needn't reach their ends.
Inputs may be any that keep to these rules, and one draw needn't show every extreme that they name: `partner`: entry (s, j) names the other copy of the same multiplier among the subdomains s - 1 (values 0 to 1023), s (1024 to 2047) and s + 1 (2048 to 3071), wrapping around over all 256 subdomains, as v mod 1024 = the copy's row. The pairing is one to one and symmetric; in every subdomain a quarter of the entries point to s - 1, a quarter to s + 1 and half inside. `elem_voxel`: value v places the element at grid row v // 128 and at column v mod 128 of the 128 columns of its subdomain's block of columns. coarse_inverse equals its transpose.
All inputs are finite; a program needn't handle non-finite values.
Results may differ from the reference program's by a relative error of at most 0.0021.
Values may be sent and summed in bfloat16 or wider, within the bound.
No kernel may reach another device: no remote copies, remote signals or barrier semaphores. Data moves between devices by JAX's collectives and lax.ppermute only.
A program may use at most 64 MiB of HBM per device.

```python
import math
import jax
import jax.numpy as jnp
import numpy as np
from jax import lax

M = 1024
C = 128
U = 1536
R = 12
EDOF = 12
ITERS = 3
SMOOTH = 2
VY = 128
SUBS = 256
NCOARSE = 3072
NE = 128
GX = 256
GY = 1024


def draw_partner(key, part):
    quarter = M // 4
    row_keys = jax.random.split(key, SUBS)
    orders = jax.vmap(lambda single_key: jax.random.permutation(single_key, M))(row_keys).astype(jnp.int32)
    following = jnp.roll(orders, -1, axis=0)
    preceding = jnp.roll(orders, 1, axis=0)
    inner = orders[:, 2 * quarter:].reshape(SUBS, -1, 2)[:, :, ::-1].reshape(SUBS, -1)
    targets = jnp.concatenate([2 * M + following[:, quarter:2 * quarter], preceding[:, :quarter], M + inner], axis=1)
    owner_ids = lax.broadcasted_iota(jnp.int32, orders.shape, 0)
    placed = jnp.zeros(orders.shape, jnp.int32).at[owner_ids, orders].set(targets)
    return placed


def draw_coarse_inverse(key, part):
    raw = jnp.clip(jax.random.normal(jax.random.fold_in(key, 17), (NCOARSE, NCOARSE), jnp.float32), -6.0, 6.0)
    return (raw + raw.T) / jnp.sqrt(2.0 * NCOARSE)


def place_ends(entries, key, least, high):
    dims = entries.shape
    place = [jax.random.randint(jax.random.fold_in(key, axis), (), 0, dims[axis]) for axis in range(len(dims))]
    entries = entries.at[tuple(place)].set(least)
    longest = dims.index(max(dims))
    place[longest] = (place[longest] + 1) % dims[longest]
    return entries.at[tuple(place)].set(high)


def block_scale(own_key, shape, pieces, smallest, top_value):
    level = 1.0
    for axis_at, parts in pieces:
        heights = jax.random.uniform(jax.random.fold_in(jax.random.fold_in(own_key, 6), axis_at), (parts,), jnp.float32, smallest / len(pieces), top_value / len(pieces))
        level = level * jnp.repeat(jnp.exp(heights), shape[axis_at] // parts).reshape((-1,) + (1,) * (len(shape) - 1 - axis_at))
    return level


def rank_table(amount, slope):
    portions = [(1 << 20) // math.isqrt(rank ** slope) + 1 for rank in range(1, amount + 1)]
    scale = 1 + sum(portions) // (1 << 30)
    return np.cumsum(np.array([max(1, weight // scale) for weight in portions]))


def ranked(key, dims, count, skew):
    table = rank_table(count, skew)
    lot = jax.random.randint(jax.random.fold_in(key, 1), dims, 0, int(table[count - 1]))
    standing = jnp.searchsorted(jnp.asarray(table, jnp.int32), lot, side="right")
    return jax.random.permutation(jax.random.fold_in(key, 2), count)[standing].astype(jnp.int32)


def bell_draw(rng, shape, spread, limit, shards=(), held_as=jnp.bfloat16):
    level = block_scale(rng, shape, shards, -0.22, 0.18) if shards else 1.0
    values = jax.random.normal(rng, shape, jnp.float32) * spread * level
    return jnp.minimum(jnp.maximum(values, -limit), limit).astype(held_as)


def setup_inputs(seed: int = 0) -> dict:
    splits = jax.random.split(jax.random.key(seed), 12)
    return {
        "dual_ops": bell_draw(splits[0], (SUBS, M, M), M ** -0.5, 0.1875, ((0, 256),)),
        "dual_rhs": bell_draw(splits[1], (SUBS, M, C), 1.0, 6.0, ((0, 256),), jnp.float32),
        "partner": draw_partner(jax.random.fold_in(splits[11], 71), 0),
        "coarse_basis": bell_draw(splits[3], (SUBS, R, M), M ** -0.5, 0.1875, ((0, 256),)),
        "coarse_inverse": draw_coarse_inverse(jax.random.fold_in(splits[11], 71), 0),
        "damping": jnp.clip(jnp.exp(jax.random.uniform(splits[5], (C,), jnp.float32, math.log(0.05), math.log(0.5))), 0.05, 0.5),
        "recovery": bell_draw(splits[6], (SUBS, U, M), M ** -0.5, 0.1875, ((0, 256),)),
        "base_disp": bell_draw(splits[7], (SUBS, U, C), 1.0, 6.0, ((0, 256),)),
        "adjoint": bell_draw(splits[8], (SUBS, U, C), 1.0, 6.0, ((0, 256),)),
        "elem_voxel": place_ends(ranked(splits[9], (SUBS, NE), GX * VY, 2), jax.random.fold_in(splits[9], 3), 0, (GX * VY) - 1).astype(jnp.int32),
        "fibre_class": place_ends(jax.random.randint(splits[10], (GX, GY), 0, 4), jax.random.fold_in(splits[10], 1), 0, 3).astype(jnp.int32),
    }


FIBRE_RATE = 0.3
ISO_RATE = 0.05
EPSILON = 1e-06

def apply_all(matrices, values):

    def single(operands):
        return jnp.dot(operands[0], operands[1], preferred_element_type=jnp.float32)
    return lax.map(single, (matrices, values))

def partner_index(partner):
    slot_rows = lax.broadcasted_iota(jnp.int32, (SUBS, M), 0)
    window_side = partner // M
    neighbour = (slot_rows + window_side - 1 + SUBS) % SUBS
    return (neighbour * M + partner % M).astype(jnp.int32).reshape(-1)

def fibre_step(smoothed, classes):
    padded = jnp.pad(smoothed, 1)
    along_rows = padded[2:, 1:-1] + padded[:-2, 1:-1] - 2.0 * smoothed
    along_cols = padded[1:-1, 2:] + padded[1:-1, :-2] - 2.0 * smoothed
    diag_main = padded[2:, 2:] + padded[:-2, :-2] - 2.0 * smoothed
    diag_anti = padded[2:, :-2] + padded[:-2, 2:] - 2.0 * smoothed
    chosen = jnp.where(classes == 0, along_rows, jnp.where(classes == 1, along_cols, jnp.where(classes == 2, diag_main, diag_anti)))
    return smoothed + FIBRE_RATE * chosen + ISO_RATE * (along_rows + along_cols)

def reference(dual_ops, dual_rhs, partner, coarse_basis, coarse_inverse, damping, recovery, base_disp, adjoint, elem_voxel, fibre_class):
    mode_basis = coarse_basis.astype(jnp.float32)
    flat_index = partner_index(partner)
    dual_iterate = jnp.zeros((SUBS, M, C), jnp.float32)
    for iteration in range(ITERS):
        images = apply_all(dual_ops, dual_iterate.astype(jnp.bfloat16)).astype(jnp.bfloat16)
        partners = jnp.take(images.reshape(SUBS * M, C), flat_index, axis=0).reshape(SUBS, M, C)
        residual = dual_rhs - (images.astype(jnp.float32) + partners.astype(jnp.float32))
        coarse_terms = jnp.einsum('sqj,sjc->sqc', mode_basis, residual, precision=lax.Precision.HIGHEST).reshape(SUBS * R, C)
        squares = lax.optimization_barrier(jnp.sum(residual * residual, axis=(0, 1)))
        correction = jnp.dot(coarse_inverse, coarse_terms, precision=lax.Precision.HIGHEST)
        step_size = damping / jnp.sqrt(squares / (SUBS * M) + EPSILON)
        projected = residual - jnp.einsum('sqj,sqc->sjc', mode_basis, correction.reshape(SUBS, R, C), precision=lax.Precision.HIGHEST)
        dual_iterate = dual_iterate + step_size[None, None, :] * projected
    multipliers = dual_iterate
    displaced = base_disp.astype(jnp.float32) - apply_all(recovery, multipliers.astype(jnp.bfloat16))
    products = (displaced * adjoint.astype(jnp.float32)).reshape(SUBS, NE, EDOF, C)
    element_grad = lax.optimization_barrier(jnp.sum(products, axis=(2, 3))) / math.sqrt(EDOF * C)
    subdomain_ids = lax.broadcasted_iota(jnp.int32, (SUBS, NE), 0)
    column_block = subdomain_ids % (GY // VY)
    grid_index = elem_voxel // VY * GY + column_block * VY + elem_voxel % VY
    smoothed = jax.ops.segment_sum(element_grad.reshape(-1), grid_index.reshape(-1).astype(jnp.int32), num_segments=GX * GY).reshape(GX, GY)
    for repeat in range(SMOOTH):
        smoothed = fibre_step(smoothed, fibre_class)
    return (multipliers, smoothed)
```

```python
import functools
import math

import jax
import jax.numpy as jnp
from jax import lax
from jax.experimental import pallas as pl
from jax.experimental.pallas import tpu as pltpu
from jax.sharding import PartitionSpec as P

EDOF = 12
MODES = 12
SUB = 32
LOAD = 8
SPOTS = 1024
COLS = 128
UNKNOWNS = 1536
EDGE = 256
MARK = 120
ENTRIES = SUB * LOAD * SPOTS
GRID_ROWS = 256
FIBRE_RATE = 0.3
ISO_RATE = 0.05
EPSILON = 1e-06

F32 = jnp.float32
BF16 = jnp.bfloat16


def call(kernel, outs, operands, name, flops=0, moved=0, limit=24, scratch=()):
    return pl.pallas_call(
        kernel,
        out_shape=[jax.ShapeDtypeStruct(shape, dtype) for shape, dtype in outs],
        scratch_shapes=list(scratch),
        compiler_params=pltpu.CompilerParams(vmem_limit_bytes=limit * 2**20),
        cost_estimate=pl.CostEstimate(flops=flops, bytes_accessed=moved, transcendentals=0),
        name=name,
    )(*operands)


def split2(value):
    high = value.astype(BF16)
    return high, (value - high.astype(F32)).astype(BF16)


def split3(value):
    high = value.astype(BF16)
    rest = value - high.astype(F32)
    middle = rest.astype(BF16)
    return high, middle, (rest - middle.astype(F32)).astype(BF16)


def dot(left, right):
    return jnp.dot(left, right, preferred_element_type=F32)


def lanes_of(shape):
    return lax.broadcasted_iota(jnp.int32, shape, 1)


def rows_of(shape):
    return lax.broadcasted_iota(jnp.int32, shape, 0)


def padded_basis(basis_ref, rows):
    basis = basis_ref[0].astype(F32)
    return jnp.concatenate([basis, jnp.zeros((rows - MODES, SPOTS), F32)], axis=0)


def coarse_rows(basis_ref, residual):
    basis = padded_basis(basis_ref, 16).astype(BF16)
    parts = dot(basis, jnp.concatenate(split3(residual), axis=1))
    terms = parts[:, :COLS] + parts[:, COLS : 2 * COLS] + parts[:, 2 * COLS :]
    squares = jnp.sum(residual * residual, axis=0, keepdims=True)
    return jnp.where(rows_of(terms.shape) == MODES, squares, terms)


def first_terms(rhs_ref, basis_ref, inverse_ref, out_ref):
    rows = coarse_rows(basis_ref, rhs_ref[0])
    inverse = jnp.concatenate([inverse_ref[...], jnp.zeros((4, SUB * LOAD * MODES), F32)], axis=0)
    inverse = jnp.concatenate([inverse, inverse[:, :128]], axis=1)
    lanes = lanes_of((16, COLS))
    mark = jnp.where((rows_of((16, COLS)) == MODES) & (lanes == MARK), 1.0, 0.0)
    for peer in range(SUB):
        start = peer * LOAD * MODES
        tile, offset = start // 128, start % 128
        piece = inverse[:, 128 * tile : 128 * tile + 256]
        if offset:
            piece = pltpu.roll(piece, 256 - offset, axis=1)
        out_ref[peer, :16, :] = rows
        out_ref[peer, 16:, :] = jnp.where(lanes < LOAD * MODES, piece[:, :128], mark)


def partial_rows(high, low, terms, out_ref):
    terms_high, terms_low = split2(terms)
    partial = dot(high, terms_high) + dot(high, terms_low) + dot(low, terms_high)
    last = jnp.concatenate([partial[MARK : MARK + 1], jnp.zeros((3, COLS), F32)], axis=0)
    for peer in range(LOAD):
        out_ref[peer] = jnp.concatenate([partial[MODES * peer : MODES * peer + MODES], last], axis=0)


def first_partial(received_ref, out_ref, block_ref):
    terms = received_ref[:, :16, :].reshape(SUB * 16, COLS)
    block = received_ref[:, 16:, :].reshape(SUB * 16, COLS).T
    high, low = split2(block)
    block_ref[:, : SUB * 16] = high
    block_ref[:, SUB * 16 :] = low
    partial_rows(high, low, terms, out_ref)


def later_partial(received_ref, block_ref, out_ref):
    terms = received_ref[...].reshape(SUB * 16, COLS)
    partial_rows(block_ref[:, : SUB * 16], block_ref[:, SUB * 16 :], terms, out_ref)


def setup(partner_ref, basis_ref, send_ref, pick_ref, lifted_ref):
    basis = padded_basis(basis_ref, COLS).T
    basis = basis + pltpu.roll(basis, 16, axis=1) + pltpu.roll(basis, 32, axis=1)
    lifted_ref[...] = basis.astype(BF16)
    partners = partner_ref[...].astype(F32)
    to_before = jnp.where(partners < SPOTS, 1.0, 0.0)
    to_after = jnp.where(partners >= 2 * SPOTS, 1.0, 0.0)
    sides = jnp.concatenate([to_before, to_after, jnp.zeros((14, SPOTS), F32)], axis=0)
    earlier = jnp.where(rows_of((SPOTS, SPOTS)) < lanes_of((SPOTS, SPOTS)), 1.0, 0.0).astype(BF16)
    place = dot(sides.astype(BF16), earlier)
    place = jnp.where(sides > 0.0, place, -1.0)
    slots = rows_of((EDGE, SPOTS)).astype(F32)
    send_ref[:EDGE, :] = jnp.where(slots == place[0:1], 1.0, 0.0).astype(BF16)
    send_ref[EDGE:, :] = jnp.where(slots == place[1:2], 1.0, 0.0).astype(BF16)
    lanes = lanes_of((128, 128)).astype(F32)
    for block in range(SPOTS // 128):
        here = slice(128 * block, 128 * block + 128)
        wanted = jnp.broadcast_to(partners[:, here], (128, 128)).T
        smaller = jnp.zeros((128, 128), F32)
        for tile in range(SPOTS // 128):
            smaller = smaller + jnp.where(partners[:, 128 * tile : 128 * tile + 128] < wanted, 1.0, 0.0)
        rank = jnp.broadcast_to(jnp.sum(smaller, axis=1, keepdims=True), (128, 128))
        for tile in range((2 * EDGE + SPOTS) // 128):
            start = 128 * tile
            if start < EDGE:
                hit = rank == lanes + start
            elif start < EDGE + SPOTS:
                hit = wanted == lanes + (start - EDGE + SPOTS)
            else:
                hit = rank == lanes + (start - EDGE - SPOTS + 3 * EDGE)
            pick_ref[here, start : start + 128] = jnp.where(hit, 1.0, 0.0).astype(BF16)


def step_parts(received_ref, damping_ref, lifted_ref):
    total = received_ref[0]
    for peer in range(1, LOAD):
        total = total + received_ref[peer]
    step = damping_ref[...] / jnp.sqrt(total[MODES : MODES + 1] / ENTRIES + EPSILON)
    correction = jnp.where(rows_of(total.shape) < MODES, total, 0.0)
    stacked = jnp.concatenate(split3(correction) + (jnp.zeros((COLS - 48, COLS), BF16),), axis=0)
    return step, dot(lifted_ref[...], stacked)


def advance(first, received_ref, damping_ref, lifted_ref, operator_ref, send_ref, residual_ref, *rest):
    step, lifted = step_parts(received_ref, damping_ref, lifted_ref)
    if first:
        iterate_ref, images_ref, down_ref, up_ref = rest
        iterate = step * (residual_ref[0] - lifted)
    else:
        before_ref, iterate_ref, images_ref, down_ref, up_ref = rest
        iterate = before_ref[...] + step * (residual_ref[...] - lifted)
    iterate_ref[...] = iterate
    images = dot(operator_ref[0], iterate.astype(BF16)).astype(BF16)
    images_ref[...] = images
    edges = dot(send_ref[...], images).astype(BF16)
    down_ref[...] = edges[:EDGE]
    up_ref[...] = edges[EDGE:]


def inner_pairs(images_ref, pick_ref, out_ref):
    out_ref[...] = dot(pick_ref[:, EDGE : EDGE + SPOTS], images_ref[...])


def residual_terms(rhs_ref, images_ref, inner_ref, pick_ref, before_ref, after_ref, basis_ref, residual_ref, out_ref):
    partners = inner_ref[...] + dot(pick_ref[:, :EDGE], before_ref[...])
    partners = partners + dot(pick_ref[:, EDGE + SPOTS :], after_ref[...])
    residual = rhs_ref[0] - (images_ref[...].astype(F32) + partners)
    residual_ref[...] = residual
    rows = coarse_rows(basis_ref, residual)
    for peer in range(SUB):
        out_ref[peer] = rows


def gradients(
    received_ref,
    damping_ref,
    lifted_ref,
    residual_ref,
    iterate_ref,
    recovery_ref,
    base_ref,
    adjoint_ref,
    voxel_ref,
    multipliers_ref,
    out_ref,
):
    step, lifted = step_parts(received_ref, damping_ref, lifted_ref)
    multipliers = iterate_ref[...] + step * (residual_ref[...] - lifted)
    multipliers_ref[0] = multipliers
    displaced = base_ref[0].astype(F32) - dot(recovery_ref[0], multipliers.astype(BF16))
    products = displaced * adjoint_ref[0].astype(F32)
    first = EDOF * rows_of((128, UNKNOWNS))
    lanes = lanes_of((128, UNKNOWNS))
    groups = jnp.where((lanes >= first) & (lanes < first + EDOF), 1.0, 0.0).astype(BF16)
    sums = dot(groups, jnp.concatenate(split2(products), axis=1))
    element = jnp.sum(sums, axis=1, keepdims=True) / math.sqrt(EDOF * COLS)
    voxel = voxel_ref[...]
    column = jnp.broadcast_to(voxel & 127, (128, 128)).astype(F32).T.astype(jnp.int32)
    placed = jnp.where(column == lanes_of((128, 128)), element, 0.0)
    rows = GRID_ROWS + 16
    at_row = jnp.where(rows_of((rows, 128)) - 2 == (voxel >> 7), 1.0, 0.0).astype(BF16)
    parts = dot(at_row, jnp.concatenate(split3(placed), axis=1))
    spread = parts[:, :COLS] + parts[:, COLS : 2 * COLS] + parts[:, 2 * COLS :]
    for peer in range(SUB):
        out_ref[peer] = spread[8 * peer : 8 * peer + 16]


def smooth(middle_ref, left_ref, right_ref, classes_ref, out_ref):
    beside = jnp.where(lanes_of((16, 128)) < 64, right_ref[...], left_ref[...])
    field = jnp.concatenate([middle_ref[...], beside], axis=1)
    classes = classes_ref[...]

    def moved(value, row, lane):
        if row:
            value = pltpu.roll(value, row % 16, axis=0)
        if lane:
            value = pltpu.roll(value, lane % 256, axis=1)
        return value

    for _ in range(2):
        twice = 2.0 * field
        up, down = moved(field, 1, 0), moved(field, -1, 0)
        along_rows = down + up - twice
        along_cols = moved(field, 0, -1) + moved(field, 0, 1) - twice
        diag_main = moved(down, 0, -1) + moved(up, 0, 1) - twice
        diag_anti = moved(down, 0, 1) + moved(up, 0, -1) - twice
        chosen = jnp.where(
            classes == 1.0,
            along_rows,
            jnp.where(classes == 2.0, along_cols, jnp.where(classes == 3.0, diag_main, diag_anti)),
        )
        field = field + FIBRE_RATE * chosen + ISO_RATE * (along_rows + along_cols)
        field = jnp.where(classes > 0.0, field, 0.0)
    out_ref[...] = field[2:10, :128]


def both_ways(value, axes, size, wrap):
    up = [(i, (i + 1) % size) for i in range(size if wrap else size - 1)]
    down = [(j, i) for i, j in up]
    return lax.ppermute(value, axes, up), lax.ppermute(value, axes, down)


def class_window(fibre_class):
    shifted = (fibre_class + 1).astype(F32)
    above, _ = both_ways(shifted[7:8], "sub", SUB, False)
    _, below = both_ways(shifted[0:1], "sub", SUB, False)
    gap = jnp.zeros((1, COLS), F32)
    middle = jnp.concatenate([gap, above, shifted, below, gap, gap, gap, gap, gap], axis=0)
    left, right = both_ways(middle, "load", LOAD, False)
    beside = jnp.where(lanes_of((16, 128)) < 64, right, left)
    return jnp.concatenate([middle, beside], axis=1)


def on_device(
    dual_ops,
    dual_rhs,
    partner,
    coarse_basis,
    coarse_inverse,
    damping,
    recovery,
    base_disp,
    adjoint,
    elem_voxel,
    fibre_class,
):
    damping = damping.reshape(1, COLS)
    tall = ((SPOTS, COLS), F32)
    to_sub = ((SUB, 16, COLS), F32)
    to_load = ((LOAD, 16, COLS), F32)
    edge = ((EDGE, COLS), BF16)
    whole = ("sub", "load")
    up = [(i, (i + 1) % (SUB * LOAD)) for i in range(SUB * LOAD)]
    down = [(j, i) for i, j in up]

    def over(value, axis):
        return lax.all_to_all(value, axis, 0, 0, tiled=True)

    (sent,) = call(
        first_terms,
        [((SUB, 32, COLS), F32)],
        (dual_rhs, coarse_basis, coarse_inverse),
        "first_terms",
    )
    received = over(sent, "sub")
    send, pick, lifted = call(
        setup,
        [((2 * EDGE, SPOTS), BF16), ((SPOTS, SPOTS + 2 * EDGE), BF16), ((SPOTS, COLS), BF16)],
        (partner, coarse_basis),
        "setup",
        flops=2 * SPOTS * SPOTS * 1024,
        moved=16 * 2**20,
    )
    partial, block = call(
        first_partial,
        [to_load, ((COLS, 2 * SUB * 16), BF16)],
        (received,),
        "first_partial",
    )
    residual = dual_rhs
    before = ()
    for iteration in range(2):
        received = over(partial, "load")
        iterate, images, lower, upper = call(
            functools.partial(advance, iteration == 0),
            [tall, ((SPOTS, COLS), BF16), edge, edge],
            (received, damping, lifted, dual_ops, send, residual) + before,
            "advance",
        )
        before = (iterate,)
        from_before = lax.ppermute(upper, whole, up)
        from_after = lax.ppermute(lower, whole, down)
        (inner,) = call(
            inner_pairs,
            [tall],
            (images, pick),
            "inner_pairs",
            flops=2 * SPOTS * SPOTS * 256,
            moved=4 * 2**20,
        )
        residual, sent = call(
            residual_terms,
            [tall, to_sub],
            (dual_rhs, images, inner, pick, from_before, from_after, coarse_basis),
            "residual_terms",
        )
        received = over(sent, "sub")
        (partial,) = call(later_partial, [to_load], (received, block), "later_partial")
    received = over(partial, "load")
    multipliers, sent = call(
        gradients,
        [((1, SPOTS, COLS), F32), to_sub],
        (received, damping, lifted, residual, iterate, recovery, base_disp, adjoint, elem_voxel),
        "gradients",
        limit=32,
    )
    middle = jnp.sum(over(sent, "sub"), axis=0)
    left, right = both_ways(middle, "load", LOAD, False)
    (field,) = call(
        smooth,
        [(fibre_class.shape, F32)],
        (middle, left, right, class_window(fibre_class)),
        "smooth",
    )
    return multipliers, field


def solution(mesh):
    placed = (
        P(("sub", "load"), None, None),
        P(("sub", "load"), None, None),
        P(("sub", "load"), None),
        P(("sub", "load"), None, None),
        P(("sub", "load"), None),
        P(),
        P(("sub", "load"), None, None),
        P(("sub", "load"), None, None),
        P(("sub", "load"), None, None),
        P(("sub", "load"), None),
        P("sub", "load"),
    )
    return jax.shard_map(
        on_device,
        mesh=mesh,
        in_specs=placed,
        out_specs=(P(("sub", "load"), None, None), P("sub", "load")),
        check_vma=False,
    )
```

```python
import functools
import math

import jax
import jax.numpy as jnp
from jax import lax
from jax.experimental import pallas as pl
from jax.experimental.pallas import tpu as pltpu
from jax.sharding import PartitionSpec as P

EDOF = 12
MODES = 12
SUB = 32
LOAD = 8
SPOTS = 1024
COLS = 128
UNKNOWNS = 1536
EDGE = 256
MARK = 120
ENTRIES = SUB * LOAD * SPOTS
GRID_ROWS = 256
FIBRE_RATE = 0.3
ISO_RATE = 0.05
EPSILON = 1e-06

F32 = jnp.float32
BF16 = jnp.bfloat16


def call(kernel, outs, operands, name, flops=0, moved=0, limit=16, scratch=()):
    return pl.pallas_call(
        kernel,
        out_shape=[jax.ShapeDtypeStruct(shape, dtype) for shape, dtype in outs],
        scratch_shapes=list(scratch),
        compiler_params=pltpu.CompilerParams(vmem_limit_bytes=limit * 2**20),
        cost_estimate=pl.CostEstimate(flops=flops, bytes_accessed=moved, transcendentals=0),
        name=name,
    )(*operands)


def split2(value):
    high = value.astype(BF16)
    return high, (value - high.astype(F32)).astype(BF16)


def split3(value):
    high = value.astype(BF16)
    rest = value - high.astype(F32)
    middle = rest.astype(BF16)
    return high, middle, (rest - middle.astype(F32)).astype(BF16)


def dot(left, right):
    return jnp.dot(left, right, preferred_element_type=F32)


def lanes_of(shape):
    return lax.broadcasted_iota(jnp.int32, shape, 1)


def rows_of(shape):
    return lax.broadcasted_iota(jnp.int32, shape, 0)


def padded_basis(basis_ref, rows):
    basis = basis_ref[0].astype(F32)
    return jnp.concatenate([basis, jnp.zeros((rows - MODES, SPOTS), F32)], axis=0)


def coarse_rows(basis_ref, residual):
    basis = padded_basis(basis_ref, 16).astype(BF16)
    parts = dot(basis, jnp.concatenate(split3(residual), axis=1))
    terms = parts[:, :COLS] + parts[:, COLS : 2 * COLS] + parts[:, 2 * COLS :]
    squares = jnp.sum(residual * residual, axis=0, keepdims=True)
    return jnp.where(rows_of(terms.shape) == MODES, squares, terms)


def first_terms(rhs_ref, basis_ref, inverse_ref, class_ref, out_ref):
    rows = coarse_rows(basis_ref, rhs_ref[0])
    classes = (class_ref[...] + 1).astype(F32)
    row = rows_of(rows.shape)
    rows = jnp.where(row == 13, classes[0:1], jnp.where(row == 14, classes[7:8], rows))
    inverse = inverse_ref[...]
    inverse = jnp.concatenate([inverse, inverse[:, :128]], axis=1)
    lanes = lanes_of((8, COLS))
    lane = lanes_of((1, COLS))
    for peer in range(SUB):
        start = peer * LOAD * MODES
        tile, offset = start // 128, start % 128
        piece = inverse[:, 128 * tile : 128 * tile + 256]
        if offset:
            piece = pltpu.roll(piece, 256 - offset, axis=1)
        piece = piece[:, :128]
        last = piece[8:12]
        beside = jnp.concatenate([pltpu.roll(last, 96, axis=1), pltpu.roll(last, 64, axis=1)], axis=0)
        spare = pltpu.roll(last[0:1], 64, axis=1)
        for place, turn in ((1, 96), (2, 0), (3, 32)):
            part = last[place : place + 1]
            spare = jnp.where(lane < 32 * place, spare, pltpu.roll(part, turn, axis=1) if turn else part)
        out_ref[peer, :16, :] = jnp.where(row == 15, spare, rows)
        out_ref[peer, 16:, :] = jnp.where(lanes < 96, piece[:8], beside)


def partial_rows(high, low, terms, out_ref):
    terms_high, terms_low = split2(terms)
    partial = dot(high, terms_high) + dot(high, terms_low) + dot(low, terms_high)
    last = jnp.concatenate([partial[MARK : MARK + 1], jnp.zeros((3, COLS), F32)], axis=0)
    for peer in range(LOAD):
        out_ref[peer] = jnp.concatenate([partial[MODES * peer : MODES * peer + MODES], last], axis=0)


def first_partial(received_ref, class_ref, out_ref, block_ref, middle_ref):
    terms = received_ref[:, :16, :].reshape(SUB * 16, COLS)
    packed = received_ref[:, 16:, :].reshape(SUB * 8, COLS)
    lanes = lanes_of((SUB * 8, COLS))
    upper = jnp.where(lanes < 96, packed, 0.0).reshape(SUB, 8, COLS)
    first = pltpu.roll(packed, 32, axis=1).reshape(SUB, 8, COLS)[:, :4]
    second = pltpu.roll(packed, 64, axis=1).reshape(SUB, 8, COLS)[:, 4:]
    spare = received_ref[:, 15, :]
    third = [pltpu.roll(spare, 64, axis=1), pltpu.roll(spare, 32, axis=1), spare, pltpu.roll(spare, 96, axis=1)]
    third = jnp.concatenate([part.reshape(SUB, 1, COLS) for part in third], axis=1)
    lanes = lax.broadcasted_iota(jnp.int32, (SUB, 4, COLS), 2)
    lower = jnp.where(lanes < 32, first, jnp.where(lanes < 64, second, jnp.where(lanes < 96, third, 0.0)))
    places = lax.broadcasted_iota(jnp.int32, (SUB, 4, COLS), 1)
    mark = jnp.where((places == 0) & (lanes == MARK), 1.0, 0.0)
    block = jnp.concatenate([upper, jnp.concatenate([lower, mark], axis=1)], axis=1)
    high, low = split2(block.reshape(SUB * 16, COLS).T)
    block_ref[:, : SUB * 16] = high
    block_ref[:, SUB * 16 :] = low
    partial_rows(high, low, terms, out_ref)
    here = lax.axis_index("sub")
    above = received_ref[jnp.maximum(here - 1, 0)][14:15]
    below = received_ref[jnp.minimum(here + 1, SUB - 1)][13:14]
    above = jnp.where(here > 0, above, 0.0)
    below = jnp.where(here < SUB - 1, below, 0.0)
    classes = (class_ref[...] + 1).astype(F32)
    gap = jnp.zeros((1, COLS), F32)
    middle = jnp.concatenate([gap, above, classes, below, gap, gap, gap, gap, gap], axis=0)
    middle_ref[...] = middle
    sides = jnp.concatenate([middle, jnp.zeros((COLS - 16, COLS), F32)], axis=0).T
    for peer in range(LOAD):
        out_ref[peer, 13:14, :] = sides[0:1]
        out_ref[peer, 14:15, :] = sides[127:128]


def later_partial(received_ref, block_ref, out_ref):
    terms = received_ref[...].reshape(SUB * 16, COLS)
    partial_rows(block_ref[:, : SUB * 16], block_ref[:, SUB * 16 :], terms, out_ref)


def setup(partner_ref, basis_ref, send_ref, pick_ref, lifted_ref):
    basis = padded_basis(basis_ref, COLS).T
    basis = basis + pltpu.roll(basis, 16, axis=1) + pltpu.roll(basis, 32, axis=1)
    lifted_ref[...] = basis.astype(BF16)
    partners = partner_ref[...].astype(F32)
    to_before = jnp.where(partners < SPOTS, 1.0, 0.0)
    to_after = jnp.where(partners >= 2 * SPOTS, 1.0, 0.0)
    sides = jnp.concatenate([to_before, to_after, jnp.zeros((14, SPOTS), F32)], axis=0)
    earlier = jnp.where(rows_of((SPOTS, SPOTS)) < lanes_of((SPOTS, SPOTS)), 1.0, 0.0).astype(BF16)
    place = dot(sides.astype(BF16), earlier)
    place = jnp.where(sides > 0.0, place, -1.0)
    slots = rows_of((EDGE, SPOTS)).astype(F32)
    send_ref[:EDGE, :] = jnp.where(slots == place[0:1], 1.0, 0.0).astype(BF16)
    send_ref[EDGE:, :] = jnp.where(slots == place[1:2], 1.0, 0.0).astype(BF16)
    lanes = lanes_of((128, 128)).astype(F32)
    for block in range(SPOTS // 128):
        here = slice(128 * block, 128 * block + 128)
        wanted = jnp.broadcast_to(partners[:, here], (128, 128)).T
        smaller = jnp.zeros((128, 128), F32)
        for tile in range(SPOTS // 128):
            smaller = smaller + jnp.where(partners[:, 128 * tile : 128 * tile + 128] < wanted, 1.0, 0.0)
        rank = jnp.broadcast_to(jnp.sum(smaller, axis=1, keepdims=True), (128, 128))
        for tile in range((2 * EDGE + SPOTS) // 128):
            start = 128 * tile
            if start < EDGE:
                hit = rank == lanes + start
            elif start < EDGE + SPOTS:
                hit = wanted == lanes + (start - EDGE + SPOTS)
            else:
                hit = rank == lanes + (start - EDGE - SPOTS + 3 * EDGE)
            pick_ref[here, start : start + 128] = jnp.where(hit, 1.0, 0.0).astype(BF16)


def step_parts(received_ref, damping_ref, lifted_ref):
    total = received_ref[0]
    for peer in range(1, LOAD):
        total = total + received_ref[peer]
    step = damping_ref[...] / jnp.sqrt(total[MODES : MODES + 1] / ENTRIES + EPSILON)
    correction = jnp.where(rows_of(total.shape) < MODES, total, 0.0)
    stacked = jnp.concatenate(split3(correction) + (jnp.zeros((COLS - 48, COLS), BF16),), axis=0)
    return step, dot(lifted_ref[...], stacked)


def advance(first, received_ref, damping_ref, lifted_ref, operator_ref, send_ref, residual_ref, *rest):
    step, lifted = step_parts(received_ref, damping_ref, lifted_ref)
    if first:
        iterate_ref, images_ref, down_ref, up_ref = rest
        iterate = step * (residual_ref[0] - lifted)
    else:
        before_ref, iterate_ref, images_ref, down_ref, up_ref = rest
        iterate = before_ref[...] + step * (residual_ref[...] - lifted)
    iterate_ref[...] = iterate
    images = dot(operator_ref[0], iterate.astype(BF16)).astype(BF16)
    images_ref[...] = images
    edges = dot(send_ref[...], images).astype(BF16)
    down_ref[...] = edges[:EDGE]
    up_ref[...] = edges[EDGE:]


def inner_pairs(images_ref, pick_ref, out_ref):
    out_ref[...] = dot(pick_ref[:, EDGE : EDGE + SPOTS], images_ref[...])


def inner_classes(images_ref, pick_ref, received_ref, middle_ref, out_ref, classes_ref):
    here = lax.axis_index("load")
    right = received_ref[jnp.minimum(here + 1, LOAD - 1)][13:14]
    left = received_ref[jnp.maximum(here - 1, 0)][14:15]
    right = jnp.where(here < LOAD - 1, right, 0.0)
    left = jnp.where(here > 0, left, 0.0)
    right = jnp.broadcast_to(right, (128, 128)).T[:16]
    left = jnp.broadcast_to(left, (128, 128)).T[:16]
    lanes = lanes_of((16, 128))
    classes_ref[:, :128] = middle_ref[...]
    classes_ref[:, 128:] = jnp.where(lanes == 0, right, jnp.where(lanes == 127, left, 0.0))
    inner_pairs(images_ref, pick_ref, out_ref)


def residual_terms(rhs_ref, images_ref, inner_ref, pick_ref, before_ref, after_ref, basis_ref, residual_ref, out_ref):
    partners = inner_ref[...] + dot(pick_ref[:, :EDGE], before_ref[...])
    partners = partners + dot(pick_ref[:, EDGE + SPOTS :], after_ref[...])
    residual = rhs_ref[0] - (images_ref[...].astype(F32) + partners)
    residual_ref[...] = residual
    rows = coarse_rows(basis_ref, residual)
    for peer in range(SUB):
        out_ref[peer] = rows


def gradients(
    received_ref,
    damping_ref,
    lifted_ref,
    residual_ref,
    iterate_ref,
    recovery_ref,
    base_ref,
    adjoint_ref,
    voxel_ref,
    multipliers_ref,
    out_ref,
):
    step, lifted = step_parts(received_ref, damping_ref, lifted_ref)
    multipliers = iterate_ref[...] + step * (residual_ref[...] - lifted)
    multipliers_ref[0] = multipliers
    displaced = base_ref[0].astype(F32) - dot(recovery_ref[0], multipliers.astype(BF16))
    products = displaced * adjoint_ref[0].astype(F32)
    first = EDOF * rows_of((128, UNKNOWNS))
    lanes = lanes_of((128, UNKNOWNS))
    groups = jnp.where((lanes >= first) & (lanes < first + EDOF), 1.0, 0.0).astype(BF16)
    sums = dot(groups, jnp.concatenate(split2(products), axis=1))
    element = jnp.sum(sums, axis=1, keepdims=True) / math.sqrt(EDOF * COLS)
    voxel = voxel_ref[...]
    column = jnp.broadcast_to(voxel & 127, (128, 128)).astype(F32).T.astype(jnp.int32)
    placed = jnp.where(column == lanes_of((128, 128)), element, 0.0)
    rows = GRID_ROWS + 16
    at_row = jnp.where(rows_of((rows, 128)) - 2 == (voxel >> 7), 1.0, 0.0).astype(BF16)
    parts = dot(at_row, jnp.concatenate(split3(placed), axis=1))
    spread = parts[:, :COLS] + parts[:, COLS : 2 * COLS] + parts[:, 2 * COLS :]
    for peer in range(SUB):
        out_ref[peer] = spread[8 * peer : 8 * peer + 16]


def smooth(middle_ref, left_ref, right_ref, classes_ref, out_ref):
    beside = jnp.where(lanes_of((16, 128)) < 64, right_ref[...], left_ref[...])
    field = jnp.concatenate([middle_ref[...], beside], axis=1)
    classes = classes_ref[...]

    def moved(value, row, lane):
        if row:
            value = pltpu.roll(value, row % 16, axis=0)
        if lane:
            value = pltpu.roll(value, lane % 256, axis=1)
        return value

    for _ in range(2):
        twice = 2.0 * field
        up, down = moved(field, 1, 0), moved(field, -1, 0)
        along_rows = down + up - twice
        along_cols = moved(field, 0, -1) + moved(field, 0, 1) - twice
        diag_main = moved(down, 0, -1) + moved(up, 0, 1) - twice
        diag_anti = moved(down, 0, 1) + moved(up, 0, -1) - twice
        chosen = jnp.where(
            classes == 1.0,
            along_rows,
            jnp.where(classes == 2.0, along_cols, jnp.where(classes == 3.0, diag_main, diag_anti)),
        )
        field = field + FIBRE_RATE * chosen + ISO_RATE * (along_rows + along_cols)
        field = jnp.where(classes > 0.0, field, 0.0)
    out_ref[...] = field[2:10, :128]


def both_ways(value, axes, size, wrap):
    up = [(i, (i + 1) % size) for i in range(size if wrap else size - 1)]
    down = [(j, i) for i, j in up]
    return lax.ppermute(value, axes, up), lax.ppermute(value, axes, down)


def on_device(
    dual_ops,
    dual_rhs,
    partner,
    coarse_basis,
    coarse_inverse,
    damping,
    recovery,
    base_disp,
    adjoint,
    elem_voxel,
    fibre_class,
):
    damping = damping.reshape(1, COLS)
    tall = ((SPOTS, COLS), F32)
    to_sub = ((SUB, 16, COLS), F32)
    to_load = ((LOAD, 16, COLS), F32)
    edge = ((EDGE, COLS), BF16)
    whole = ("sub", "load")
    up = [(i, (i + 1) % (SUB * LOAD)) for i in range(SUB * LOAD)]
    down = [(j, i) for i, j in up]

    def over(value, axis):
        return lax.all_to_all(value, axis, 0, 0, tiled=True)

    (sent,) = call(
        first_terms,
        [((SUB, 24, COLS), F32)],
        (dual_rhs, coarse_basis, coarse_inverse, fibre_class),
        "first_terms",
    )
    received = over(sent, "sub")
    send, pick, lifted = call(
        setup,
        [((2 * EDGE, SPOTS), BF16), ((SPOTS, SPOTS + 2 * EDGE), BF16), ((SPOTS, COLS), BF16)],
        (partner, coarse_basis),
        "setup",
        flops=2 * SPOTS * SPOTS * 1024,
        moved=16 * 2**20,
    )
    partial, block, middle = call(
        first_partial,
        [to_load, ((COLS, 2 * SUB * 16), BF16), ((16, COLS), F32)],
        (received, fibre_class),
        "first_partial",
    )
    residual = dual_rhs
    before = ()
    for iteration in range(2):
        received = over(partial, "load")
        iterate, images, lower, upper = call(
            functools.partial(advance, iteration == 0),
            [tall, ((SPOTS, COLS), BF16), edge, edge],
            (received, damping, lifted, dual_ops, send, residual) + before,
            "advance",
        )
        before = (iterate,)
        from_before = lax.ppermute(upper, whole, up)
        from_after = lax.ppermute(lower, whole, down)
        more = (received, middle) if iteration == 0 else ()
        inner = call(
            inner_pairs if iteration else inner_classes,
            [tall] if iteration else [tall, ((16, 2 * COLS), F32)],
            (images, pick) + more,
            "inner_pairs",
            flops=2 * SPOTS * SPOTS * 256,
            moved=4 * 2**20,
        )
        if iteration == 0:
            classes = inner[1]
        inner = inner[0]
        residual, sent = call(
            residual_terms,
            [tall, to_sub],
            (dual_rhs, images, inner, pick, from_before, from_after, coarse_basis),
            "residual_terms",
        )
        received = over(sent, "sub")
        (partial,) = call(later_partial, [to_load], (received, block), "later_partial")
    received = over(partial, "load")
    multipliers, sent = call(
        gradients,
        [((1, SPOTS, COLS), F32), to_sub],
        (received, damping, lifted, residual, iterate, recovery, base_disp, adjoint, elem_voxel),
        "gradients",
    )
    middle = jnp.sum(over(sent, "sub"), axis=0)
    left, right = both_ways(middle, "load", LOAD, False)
    (field,) = call(
        smooth,
        [(fibre_class.shape, F32)],
        (middle, left, right, classes),
        "smooth",
    )
    return multipliers, field


def solution(mesh):
    placed = (
        P(("sub", "load"), None, None),
        P(("sub", "load"), None, None),
        P(("sub", "load"), None),
        P(("sub", "load"), None, None),
        P(("sub", "load"), None),
        P(),
        P(("sub", "load"), None, None),
        P(("sub", "load"), None, None),
        P(("sub", "load"), None, None),
        P(("sub", "load"), None),
        P("sub", "load"),
    )
    return jax.shard_map(
        on_device,
        mesh=mesh,
        in_specs=placed,
        out_specs=(P(("sub", "load"), None, None), P("sub", "load")),
        check_vma=False,
    )
```

```python
import functools
import math

import jax
import jax.numpy as jnp
from jax import lax
from jax.experimental import pallas as pl
from jax.experimental.pallas import tpu as pltpu
from jax.sharding import PartitionSpec as P

EDOF = 12
MODES = 12
SUB = 32
LOAD = 8
SPOTS = 1024
COLS = 128
UNKNOWNS = 1536
EDGE = 256
MARK = 120
FIRST = 16
ENTRIES = SUB * LOAD * SPOTS
GRID_ROWS = 256
FIBRE_RATE = 0.3
ISO_RATE = 0.05
EPSILON = 1e-06

F32 = jnp.float32
BF16 = jnp.bfloat16


def call(kernel, outs, operands, name, flops=0, moved=16 * 2**20, limit=16, scratch=(), far=()):
    vmem, hbm = pl.BlockSpec(memory_space=pltpu.VMEM), pl.BlockSpec(memory_space=pltpu.HBM)
    return pl.pallas_call(
        kernel,
        in_specs=[hbm if place in far else vmem for place in range(len(operands))],
        out_shape=[jax.ShapeDtypeStruct(shape, dtype) for shape, dtype in outs],
        scratch_shapes=list(scratch),
        compiler_params=pltpu.CompilerParams(vmem_limit_bytes=int(limit * 2**20)),
        cost_estimate=pl.CostEstimate(flops=flops, bytes_accessed=moved, transcendentals=0),
        name=name,
    )(*operands)


def split2(value):
    high = value.astype(BF16)
    return high, (value - high.astype(F32)).astype(BF16)


def split3(value):
    high = value.astype(BF16)
    rest = value - high.astype(F32)
    middle = rest.astype(BF16)
    return high, middle, (rest - middle.astype(F32)).astype(BF16)


def dot(left, right):
    return jnp.dot(left, right, preferred_element_type=F32)


def lanes_of(shape):
    return lax.broadcasted_iota(jnp.int32, shape, 1)


def rows_of(shape):
    return lax.broadcasted_iota(jnp.int32, shape, 0)


def padded_basis(basis_ref, rows):
    basis = basis_ref[0].astype(F32)
    return jnp.concatenate([basis, jnp.zeros((rows - MODES, SPOTS), F32)], axis=0)


def coarse_rows(basis_ref, residual):
    basis = padded_basis(basis_ref, 16).astype(BF16)
    parts = dot(basis, jnp.concatenate(split3(residual), axis=1))
    terms = parts[:, :COLS] + parts[:, COLS : 2 * COLS] + parts[:, 2 * COLS :]
    squares = jnp.sum(residual * residual, axis=0, keepdims=True)
    return jnp.where(rows_of(terms.shape) == MODES, squares, terms)


def first_terms(
    rhs_hbm,
    basis_hbm,
    inverse_hbm,
    partner_hbm,
    out_ref,
    send_ref,
    lifted_ref,
    rhs_ref,
    basis_ref,
    inverse_ref,
    partner_ref,
    rhs_sem,
    basis_sem,
    inverse_sem,
    partner_sem,
):
    copies = [
        pltpu.make_async_copy(inverse_hbm, inverse_ref, inverse_sem),
        pltpu.make_async_copy(basis_hbm, basis_ref, basis_sem),
        pltpu.make_async_copy(rhs_hbm, rhs_ref, rhs_sem),
        pltpu.make_async_copy(partner_hbm, partner_ref, partner_sem),
    ]
    for copy in copies:
        copy.start()
    copies[0].wait()
    inverse = inverse_ref[...]
    inverse = jnp.concatenate([inverse, inverse[:, :128]], axis=1)
    lanes = lanes_of((8, COLS))
    lane = lanes_of((1, COLS))
    spares = []
    for peer in range(SUB):
        start = peer * LOAD * MODES
        tile, offset = start // 128, start % 128
        piece = inverse[:, 128 * tile : 128 * tile + 256]
        if offset:
            piece = pltpu.roll(piece, 256 - offset, axis=1)
        piece = piece[:, :128]
        last = piece[8:12]
        beside = jnp.concatenate([pltpu.roll(last, 96, axis=1), pltpu.roll(last, 64, axis=1)], axis=0)
        spare = pltpu.roll(last[0:1], 64, axis=1)
        for place, turn in ((1, 96), (2, 0), (3, 32)):
            part = last[place : place + 1]
            spare = jnp.where(lane < 32 * place, spare, pltpu.roll(part, turn, axis=1) if turn else part)
        out_ref[peer, 16:, :] = jnp.where(lanes < 96, piece[:8], beside)
        spares.append(spare)
    copies[3].wait()
    edge_rows(partner_ref[...].astype(F32), send_ref)
    copies[1].wait()
    basis = padded_basis(basis_ref, COLS).T
    basis = basis + pltpu.roll(basis, 16, axis=1) + pltpu.roll(basis, 32, axis=1)
    lifted_ref[...] = basis.astype(BF16)
    copies[2].wait()
    rows = coarse_rows(basis_ref, rhs_ref[0])
    row = rows_of(rows.shape)
    for peer in range(SUB):
        out_ref[peer, :16, :] = jnp.where(row == 15, spares[peer], rows)


def partial_rows(high, low, terms, out_ref):
    terms_high, terms_low = split2(terms)
    partial = dot(high, terms_high) + dot(high, terms_low) + dot(low, terms_high)
    last = jnp.concatenate([partial[MARK : MARK + 1], jnp.zeros((3, COLS), F32)], axis=0)
    for peer in range(LOAD):
        out_ref[peer] = jnp.concatenate([partial[MODES * peer : MODES * peer + MODES], last], axis=0)


def first_partial(received_ref, out_ref, block_ref):
    terms = received_ref[:, :16, :].reshape(SUB * 16, COLS)
    packed = received_ref[:, 16:, :].reshape(SUB * 8, COLS)
    lanes = lanes_of((SUB * 8, COLS))
    upper = jnp.where(lanes < 96, packed, 0.0).reshape(SUB, 8, COLS)
    first = pltpu.roll(packed, 32, axis=1).reshape(SUB, 8, COLS)[:, :4]
    second = pltpu.roll(packed, 64, axis=1).reshape(SUB, 8, COLS)[:, 4:]
    spare = received_ref[:, 15, :]
    third = [pltpu.roll(spare, 64, axis=1), pltpu.roll(spare, 32, axis=1), spare, pltpu.roll(spare, 96, axis=1)]
    third = jnp.concatenate([part.reshape(SUB, 1, COLS) for part in third], axis=1)
    lanes = lax.broadcasted_iota(jnp.int32, (SUB, 4, COLS), 2)
    lower = jnp.where(lanes < 32, first, jnp.where(lanes < 64, second, jnp.where(lanes < 96, third, 0.0)))
    places = lax.broadcasted_iota(jnp.int32, (SUB, 4, COLS), 1)
    mark = jnp.where((places == 0) & (lanes == MARK), 1.0, 0.0)
    block = jnp.concatenate([upper, jnp.concatenate([lower, mark], axis=1)], axis=1)
    high, low = split2(block.reshape(SUB * 16, COLS).T)
    block_ref[:, : SUB * 16] = high
    block_ref[:, SUB * 16 :] = low
    partial_rows(high, low, terms, out_ref)


def later_partial(received_ref, block_ref, out_ref):
    terms = received_ref[...].reshape(SUB * 16, COLS)
    partial_rows(block_ref[:, : SUB * 16], block_ref[:, SUB * 16 :], terms, out_ref)


def class_partial(received_ref, block_ref, class_ref, out_ref, middle_ref):
    later_partial(received_ref, block_ref, out_ref)
    here = lax.axis_index("sub")
    above = received_ref[jnp.maximum(here - 1, 0)][14:15]
    below = received_ref[jnp.minimum(here + 1, SUB - 1)][13:14]
    above = jnp.where(here > 0, above, 0.0)
    below = jnp.where(here < SUB - 1, below, 0.0)
    classes = (class_ref[...] + 1).astype(F32)
    gap = jnp.zeros((1, COLS), F32)
    middle = jnp.concatenate([gap, above, classes, below, gap, gap, gap, gap, gap], axis=0)
    middle_ref[...] = middle
    sides = jnp.concatenate([middle, jnp.zeros((COLS - 16, COLS), F32)], axis=0).T
    for peer in range(LOAD):
        out_ref[peer, 13:14, :] = sides[0:1]
        out_ref[peer, 14:15, :] = sides[127:128]


def edge_rows(partners, send_ref):
    to_before = jnp.where(partners < SPOTS, 1.0, 0.0)
    to_after = jnp.where(partners >= 2 * SPOTS, 1.0, 0.0)
    sides = jnp.concatenate([to_before, to_after, jnp.zeros((14, SPOTS), F32)], axis=0)
    earlier = jnp.where(rows_of((SPOTS, SPOTS)) < lanes_of((SPOTS, SPOTS)), 1.0, 0.0).astype(BF16)
    place = dot(sides.astype(BF16), earlier)
    place = jnp.where(sides > 0.0, place, -1.0)
    slots = rows_of((EDGE, SPOTS)).astype(F32)
    send_ref[:EDGE, :] = jnp.where(slots == place[0:1], 1.0, 0.0).astype(BF16)
    send_ref[EDGE:, :] = jnp.where(slots == place[1:2], 1.0, 0.0).astype(BF16)


def first_inner(images_ref, partner_ref, out_ref, pick_ref):
    partners = partner_ref[...].astype(F32)
    lanes = lanes_of((128, 128)).astype(F32)
    for block in range(SPOTS // 128):
        here = slice(128 * block, 128 * block + 128)
        wanted = jnp.broadcast_to(partners[:, here], (128, 128)).T
        smaller = jnp.zeros((128, 128), F32)
        for tile in range(SPOTS // 128):
            smaller = smaller + jnp.where(partners[:, 128 * tile : 128 * tile + 128] < wanted, 1.0, 0.0)
        rank = jnp.broadcast_to(jnp.sum(smaller, axis=1, keepdims=True), (128, 128))
        for tile in range((2 * EDGE + SPOTS) // 128):
            start = 128 * tile
            if start < EDGE:
                hit = rank == lanes + start
            elif start < EDGE + SPOTS:
                hit = wanted == lanes + (start - EDGE + SPOTS)
            else:
                hit = rank == lanes + (start - EDGE - SPOTS + 3 * EDGE)
            pick_ref[here, start : start + 128] = jnp.where(hit, 1.0, 0.0).astype(BF16)
    inner_pairs(images_ref, pick_ref, out_ref)


def step_parts(received_ref, damping_ref, lifted_ref):
    total = received_ref[0]
    for peer in range(1, LOAD):
        total = total + received_ref[peer]
    step = damping_ref[...] / jnp.sqrt(total[MODES : MODES + 1] / ENTRIES + EPSILON)
    correction = jnp.where(rows_of(total.shape) < MODES, total, 0.0)
    stacked = jnp.concatenate(split3(correction) + (jnp.zeros((COLS - 48, COLS), BF16),), axis=0)
    return step, dot(lifted_ref[...], stacked)


def advance(first, received_ref, damping_ref, lifted_ref, operator_ref, send_ref, residual_ref, *rest):
    step, lifted = step_parts(received_ref, damping_ref, lifted_ref)
    if first:
        iterate_ref, images_ref, down_ref, up_ref = rest
        iterate = step * (residual_ref[0] - lifted)
    else:
        before_ref, iterate_ref, images_ref, down_ref, up_ref = rest
        iterate = before_ref[...] + step * (residual_ref[...] - lifted)
    iterate_ref[...] = iterate
    images = dot(operator_ref[0], iterate.astype(BF16)).astype(BF16)
    images_ref[...] = images
    edges = dot(send_ref[...], images).astype(BF16)
    down_ref[...] = edges[:EDGE]
    up_ref[...] = edges[EDGE:]


def inner_pairs(images_ref, pick_ref, out_ref):
    out_ref[...] = dot(pick_ref[:, EDGE : EDGE + SPOTS], images_ref[...])


def inner_classes(images_ref, pick_ref, received_ref, middle_ref, out_ref, classes_ref):
    here = lax.axis_index("load")
    right = received_ref[jnp.minimum(here + 1, LOAD - 1)][13:14]
    left = received_ref[jnp.maximum(here - 1, 0)][14:15]
    right = jnp.where(here < LOAD - 1, right, 0.0)
    left = jnp.where(here > 0, left, 0.0)
    right = jnp.broadcast_to(right, (128, 128)).T[:16]
    left = jnp.broadcast_to(left, (128, 128)).T[:16]
    lanes = lanes_of((16, 128))
    classes_ref[:, :128] = middle_ref[...]
    classes_ref[:, 128:] = jnp.where(lanes == 0, right, jnp.where(lanes == 127, left, 0.0))
    inner_pairs(images_ref, pick_ref, out_ref)


def residual_terms(
    rhs_ref, images_ref, inner_ref, pick_ref, before_ref, after_ref, basis_ref, class_ref, residual_ref, out_ref
):
    partners = inner_ref[...] + dot(pick_ref[:, :EDGE], before_ref[...])
    partners = partners + dot(pick_ref[:, EDGE + SPOTS :], after_ref[...])
    residual = rhs_ref[0] - (images_ref[...].astype(F32) + partners)
    residual_ref[...] = residual
    rows = coarse_rows(basis_ref, residual)
    classes = (class_ref[...] + 1).astype(F32)
    row = rows_of(rows.shape)
    rows = jnp.where(row == 13, classes[0:1], jnp.where(row == 14, classes[7:8], rows))
    for peer in range(SUB):
        out_ref[peer] = rows


def gradients(
    received_ref,
    damping_ref,
    lifted_ref,
    residual_ref,
    iterate_ref,
    recovery_ref,
    base_ref,
    adjoint_ref,
    voxel_ref,
    multipliers_ref,
    out_ref,
):
    step, lifted = step_parts(received_ref, damping_ref, lifted_ref)
    multipliers = iterate_ref[...] + step * (residual_ref[...] - lifted)
    multipliers_ref[0] = multipliers
    displaced = base_ref[0].astype(F32) - dot(recovery_ref[0], multipliers.astype(BF16))
    products = displaced * adjoint_ref[0].astype(F32)
    first = EDOF * rows_of((128, UNKNOWNS))
    lanes = lanes_of((128, UNKNOWNS))
    groups = jnp.where((lanes >= first) & (lanes < first + EDOF), 1.0, 0.0).astype(BF16)
    sums = dot(groups, jnp.concatenate(split2(products), axis=1))
    element = jnp.sum(sums, axis=1, keepdims=True) / math.sqrt(EDOF * COLS)
    voxel = voxel_ref[...]
    column = jnp.broadcast_to(voxel & 127, (128, 128)).astype(F32).T.astype(jnp.int32)
    placed = jnp.where(column == lanes_of((128, 128)), element, 0.0)
    rows = GRID_ROWS + 16
    at_row = jnp.where(rows_of((rows, 128)) - 2 == (voxel >> 7), 1.0, 0.0).astype(BF16)
    parts = dot(at_row, jnp.concatenate(split3(placed), axis=1))
    spread = parts[:, :COLS] + parts[:, COLS : 2 * COLS] + parts[:, 2 * COLS :]
    for peer in range(SUB):
        out_ref[peer] = spread[8 * peer : 8 * peer + 16]


def smooth(middle_ref, left_ref, right_ref, classes_ref, out_ref):
    beside = jnp.where(lanes_of((16, 128)) < 64, right_ref[...], left_ref[...])
    field = jnp.concatenate([middle_ref[...], beside], axis=1)
    classes = classes_ref[...]

    def moved(value, row, lane):
        if row:
            value = pltpu.roll(value, row % 16, axis=0)
        if lane:
            value = pltpu.roll(value, lane % 256, axis=1)
        return value

    for _ in range(2):
        twice = 2.0 * field
        up, down = moved(field, 1, 0), moved(field, -1, 0)
        along_rows = down + up - twice
        along_cols = moved(field, 0, -1) + moved(field, 0, 1) - twice
        diag_main = moved(down, 0, -1) + moved(up, 0, 1) - twice
        diag_anti = moved(down, 0, 1) + moved(up, 0, -1) - twice
        chosen = jnp.where(
            classes == 1.0,
            along_rows,
            jnp.where(classes == 2.0, along_cols, jnp.where(classes == 3.0, diag_main, diag_anti)),
        )
        field = field + FIBRE_RATE * chosen + ISO_RATE * (along_rows + along_cols)
        field = jnp.where(classes > 0.0, field, 0.0)
    out_ref[...] = field[2:10, :128]


def both_ways(value, axes, size, wrap):
    up = [(i, (i + 1) % size) for i in range(size if wrap else size - 1)]
    down = [(j, i) for i, j in up]
    return lax.ppermute(value, axes, up), lax.ppermute(value, axes, down)


def on_device(
    dual_ops,
    dual_rhs,
    partner,
    coarse_basis,
    coarse_inverse,
    damping,
    recovery,
    base_disp,
    adjoint,
    elem_voxel,
    fibre_class,
):
    damping = damping.reshape(1, COLS)
    tall = ((SPOTS, COLS), F32)
    to_sub = ((SUB, 16, COLS), F32)
    to_load = ((LOAD, 16, COLS), F32)
    edge = ((EDGE, COLS), BF16)
    whole = ("sub", "load")
    up = [(i, (i + 1) % (SUB * LOAD)) for i in range(SUB * LOAD)]
    down = [(j, i) for i, j in up]

    def over(value, axis):
        return lax.all_to_all(value, axis, 0, 0, tiled=True)

    sent, send, lifted = call(
        first_terms,
        [((SUB, 24, COLS), F32), ((2 * EDGE, SPOTS), BF16), ((SPOTS, COLS), BF16)],
        (dual_rhs, coarse_basis, coarse_inverse, partner),
        "first_terms",
        scratch=[
            pltpu.VMEM(dual_rhs.shape, F32),
            pltpu.VMEM(coarse_basis.shape, BF16),
            pltpu.VMEM(coarse_inverse.shape, F32),
            pltpu.VMEM(partner.shape, jnp.int32),
        ]
        + [pltpu.SemaphoreType.DMA] * 4,
        far=(0, 1, 2, 3),
        limit=FIRST,
    )
    received = over(sent, "sub")
    partial, block = call(
        first_partial,
        [to_load, ((COLS, 2 * SUB * 16), BF16)],
        (received,),
        "first_partial",
    )
    residual = dual_rhs
    before = ()
    for iteration in range(2):
        received = over(partial, "load")
        iterate, images, lower, upper = call(
            functools.partial(advance, iteration == 0),
            [tall, ((SPOTS, COLS), BF16), edge, edge],
            (received, damping, lifted, dual_ops, send, residual) + before,
            "advance",
        )
        before = (iterate,)
        from_before = lax.ppermute(upper, whole, up)
        from_after = lax.ppermute(lower, whole, down)
        if iteration == 0:
            inner, pick = call(
                first_inner, [tall, ((SPOTS, SPOTS + 2 * EDGE), BF16)], (images, partner), "first_inner",
                flops=2 * SPOTS * SPOTS * 1024, moved=8 * 2**20,
            )
        else:
            inner, classes = call(
                inner_classes, [tall, ((16, 2 * COLS), F32)], (images, pick, received, middle), "inner_classes",
                flops=2 * SPOTS * SPOTS * 256, moved=4 * 2**20,
            )
        residual, sent = call(
            residual_terms,
            [tall, to_sub],
            (dual_rhs, images, inner, pick, from_before, from_after, coarse_basis, fibre_class),
            "residual_terms",
        )
        received = over(sent, "sub")
        if iteration == 0:
            partial, middle = call(
                class_partial, [to_load, ((16, COLS), F32)], (received, block, fibre_class), "class_partial"
            )
        else:
            (partial,) = call(later_partial, [to_load], (received, block), "later_partial")
    received = over(partial, "load")
    multipliers, sent = call(
        gradients,
        [((1, SPOTS, COLS), F32), to_sub],
        (received, damping, lifted, residual, iterate, recovery, base_disp, adjoint, elem_voxel),
        "gradients",
    )
    middle = jnp.sum(over(sent, "sub"), axis=0)
    left, right = both_ways(middle, "load", LOAD, False)
    (field,) = call(
        smooth,
        [(fibre_class.shape, F32)],
        (middle, left, right, classes),
        "smooth",
    )
    return multipliers, field


def solution(mesh):
    placed = (
        P(("sub", "load"), None, None),
        P(("sub", "load"), None, None),
        P(("sub", "load"), None),
        P(("sub", "load"), None, None),
        P(("sub", "load"), None),
        P(),
        P(("sub", "load"), None, None),
        P(("sub", "load"), None, None),
        P(("sub", "load"), None, None),
        P(("sub", "load"), None),
        P("sub", "load"),
    )
    return jax.shard_map(
        on_device,
        mesh=mesh,
        in_specs=placed,
        out_specs=(P(("sub", "load"), None, None), P("sub", "load")),
        check_vma=False,
    )
```

```python
import functools
import math

import jax
import jax.numpy as jnp
from jax import lax
from jax.experimental import pallas as pl
from jax.experimental.pallas import tpu as pltpu
from jax.sharding import PartitionSpec as P

EDOF = 12
MODES = 12
SUB = 32
LOAD = 8
SPOTS = 1024
COLS = 128
UNKNOWNS = 1536
EDGE = 256
MARK = 120
FIRST = 60
PART = 40
ENTRIES = SUB * LOAD * SPOTS
GRID_ROWS = 256
FIBRE_RATE = 0.3
ISO_RATE = 0.05
EPSILON = 1e-06

F32 = jnp.float32
BF16 = jnp.bfloat16


def call(kernel, outs, operands, name, flops=0, moved=16 * 2**20, limit=16, scratch=(), far=()):
    vmem, hbm = pl.BlockSpec(memory_space=pltpu.VMEM), pl.BlockSpec(memory_space=pltpu.HBM)
    return pl.pallas_call(
        kernel,
        in_specs=[hbm if place in far else vmem for place in range(len(operands))],
        out_shape=[jax.ShapeDtypeStruct(shape, dtype) for shape, dtype in outs],
        scratch_shapes=list(scratch),
        compiler_params=pltpu.CompilerParams(vmem_limit_bytes=int(limit * 2**20)),
        cost_estimate=pl.CostEstimate(flops=flops, bytes_accessed=moved, transcendentals=0),
        name=name,
    )(*operands)


def split2(value):
    high = value.astype(BF16)
    return high, (value - high.astype(F32)).astype(BF16)


def split3(value):
    high = value.astype(BF16)
    rest = value - high.astype(F32)
    middle = rest.astype(BF16)
    return high, middle, (rest - middle.astype(F32)).astype(BF16)


def dot(left, right):
    return jnp.dot(left, right, preferred_element_type=F32)


def lanes_of(shape):
    return lax.broadcasted_iota(jnp.int32, shape, 1)


def rows_of(shape):
    return lax.broadcasted_iota(jnp.int32, shape, 0)


def padded_basis(basis_ref, rows):
    basis = basis_ref[0].astype(F32)
    return jnp.concatenate([basis, jnp.zeros((rows - MODES, SPOTS), F32)], axis=0)


def coarse_rows(basis_ref, residual):
    basis = padded_basis(basis_ref, 16).astype(BF16)
    parts = dot(basis, jnp.concatenate(split3(residual), axis=1))
    terms = parts[:, :COLS] + parts[:, COLS : 2 * COLS] + parts[:, 2 * COLS :]
    squares = jnp.sum(residual * residual, axis=0, keepdims=True)
    return jnp.where(rows_of(terms.shape) == MODES, squares, terms)


def first_terms(
    rhs_hbm,
    basis_hbm,
    inverse_hbm,
    partner_hbm,
    out_ref,
    send_ref,
    lifted_ref,
    rhs_ref,
    basis_ref,
    inverse_ref,
    partner_ref,
    rhs_sem,
    basis_sem,
    inverse_sem,
    partner_sem,
):
    copies = [
        pltpu.make_async_copy(inverse_hbm, inverse_ref, inverse_sem),
        pltpu.make_async_copy(basis_hbm, basis_ref, basis_sem),
        pltpu.make_async_copy(rhs_hbm, rhs_ref, rhs_sem),
        pltpu.make_async_copy(partner_hbm, partner_ref, partner_sem),
    ]
    for copy in copies:
        copy.start()
    copies[0].wait()
    inverse = inverse_ref[...]
    inverse = jnp.concatenate([inverse, inverse[:, :128]], axis=1)
    lanes = lanes_of((8, COLS))
    lane = lanes_of((1, COLS))
    spares = []
    for peer in range(SUB):
        start = peer * LOAD * MODES
        tile, offset = start // 128, start % 128
        piece = inverse[:, 128 * tile : 128 * tile + 256]
        if offset:
            piece = pltpu.roll(piece, 256 - offset, axis=1)
        piece = piece[:, :128]
        last = piece[8:12]
        beside = jnp.concatenate([pltpu.roll(last, 96, axis=1), pltpu.roll(last, 64, axis=1)], axis=0)
        spare = pltpu.roll(last[0:1], 64, axis=1)
        for place, turn in ((1, 96), (2, 0), (3, 32)):
            part = last[place : place + 1]
            spare = jnp.where(lane < 32 * place, spare, pltpu.roll(part, turn, axis=1) if turn else part)
        out_ref[peer, 16:, :] = jnp.where(lanes < 96, piece[:8], beside)
        spares.append(spare)
    copies[3].wait()
    edge_rows(partner_ref[...].astype(F32), send_ref)
    copies[1].wait()
    basis = padded_basis(basis_ref, COLS).T
    basis = basis + pltpu.roll(basis, 16, axis=1) + pltpu.roll(basis, 32, axis=1)
    lifted_ref[...] = basis.astype(BF16)
    copies[2].wait()
    rows = coarse_rows(basis_ref, rhs_ref[0])
    row = rows_of(rows.shape)
    for peer in range(SUB):
        out_ref[peer, :16, :] = jnp.where(row == 15, spares[peer], rows)


def partial_rows(high, low, terms, out_ref):
    terms_high, terms_low = split2(terms)
    partial = dot(high, terms_high) + dot(high, terms_low) + dot(low, terms_high)
    last = jnp.concatenate([partial[MARK : MARK + 1], jnp.zeros((3, COLS), F32)], axis=0)
    for peer in range(LOAD):
        out_ref[peer] = jnp.concatenate([partial[MODES * peer : MODES * peer + MODES], last], axis=0)


def first_partial(
    received_ref, operator_hbm, rhs_hbm, out_ref, block_ref, operator_ref, rhs_ref, operator_sem, rhs_sem
):
    copies = [
        pltpu.make_async_copy(operator_hbm, operator_ref, operator_sem),
        pltpu.make_async_copy(rhs_hbm, rhs_ref, rhs_sem),
    ]
    for copy in copies:
        copy.start()
    terms = received_ref[:, :16, :].reshape(SUB * 16, COLS)
    packed = received_ref[:, 16:, :].reshape(SUB * 8, COLS)
    lanes = lanes_of((SUB * 8, COLS))
    upper = jnp.where(lanes < 96, packed, 0.0).reshape(SUB, 8, COLS)
    first = pltpu.roll(packed, 32, axis=1).reshape(SUB, 8, COLS)[:, :4]
    second = pltpu.roll(packed, 64, axis=1).reshape(SUB, 8, COLS)[:, 4:]
    spare = received_ref[:, 15, :]
    third = [pltpu.roll(spare, 64, axis=1), pltpu.roll(spare, 32, axis=1), spare, pltpu.roll(spare, 96, axis=1)]
    third = jnp.concatenate([part.reshape(SUB, 1, COLS) for part in third], axis=1)
    lanes = lax.broadcasted_iota(jnp.int32, (SUB, 4, COLS), 2)
    lower = jnp.where(lanes < 32, first, jnp.where(lanes < 64, second, jnp.where(lanes < 96, third, 0.0)))
    places = lax.broadcasted_iota(jnp.int32, (SUB, 4, COLS), 1)
    mark = jnp.where((places == 0) & (lanes == MARK), 1.0, 0.0)
    block = jnp.concatenate([upper, jnp.concatenate([lower, mark], axis=1)], axis=1)
    high, low = split2(block.reshape(SUB * 16, COLS).T)
    block_ref[:, : SUB * 16] = high
    block_ref[:, SUB * 16 :] = low
    partial_rows(high, low, terms, out_ref)
    for copy in copies:
        copy.wait()


def later_partial(received_ref, block_ref, out_ref):
    terms = received_ref[...].reshape(SUB * 16, COLS)
    partial_rows(block_ref[:, : SUB * 16], block_ref[:, SUB * 16 :], terms, out_ref)


def class_partial(received_ref, block_ref, class_ref, out_ref, middle_ref):
    later_partial(received_ref, block_ref, out_ref)
    here = lax.axis_index("sub")
    above = received_ref[jnp.maximum(here - 1, 0)][14:15]
    below = received_ref[jnp.minimum(here + 1, SUB - 1)][13:14]
    above = jnp.where(here > 0, above, 0.0)
    below = jnp.where(here < SUB - 1, below, 0.0)
    classes = (class_ref[...] + 1).astype(F32)
    gap = jnp.zeros((1, COLS), F32)
    middle = jnp.concatenate([gap, above, classes, below, gap, gap, gap, gap, gap], axis=0)
    middle_ref[...] = middle
    sides = jnp.concatenate([middle, jnp.zeros((COLS - 16, COLS), F32)], axis=0).T
    for peer in range(LOAD):
        out_ref[peer, 13:14, :] = sides[0:1]
        out_ref[peer, 14:15, :] = sides[127:128]


def edge_rows(partners, send_ref):
    to_before = jnp.where(partners < SPOTS, 1.0, 0.0)
    to_after = jnp.where(partners >= 2 * SPOTS, 1.0, 0.0)
    sides = jnp.concatenate([to_before, to_after, jnp.zeros((14, SPOTS), F32)], axis=0)
    earlier = jnp.where(rows_of((SPOTS, SPOTS)) < lanes_of((SPOTS, SPOTS)), 1.0, 0.0).astype(BF16)
    place = dot(sides.astype(BF16), earlier)
    place = jnp.where(sides > 0.0, place, -1.0)
    slots = rows_of((EDGE, SPOTS)).astype(F32)
    send_ref[:EDGE, :] = jnp.where(slots == place[0:1], 1.0, 0.0).astype(BF16)
    send_ref[EDGE:, :] = jnp.where(slots == place[1:2], 1.0, 0.0).astype(BF16)


def first_inner(images_ref, partner_ref, out_ref, pick_ref):
    partners = partner_ref[...].astype(F32)
    lanes = lanes_of((128, 128)).astype(F32)
    for block in range(SPOTS // 128):
        here = slice(128 * block, 128 * block + 128)
        wanted = jnp.broadcast_to(partners[:, here], (128, 128)).T
        smaller = jnp.zeros((128, 128), F32)
        for tile in range(SPOTS // 128):
            smaller = smaller + jnp.where(partners[:, 128 * tile : 128 * tile + 128] < wanted, 1.0, 0.0)
        rank = jnp.broadcast_to(jnp.sum(smaller, axis=1, keepdims=True), (128, 128))
        for tile in range((2 * EDGE + SPOTS) // 128):
            start = 128 * tile
            if start < EDGE:
                hit = rank == lanes + start
            elif start < EDGE + SPOTS:
                hit = wanted == lanes + (start - EDGE + SPOTS)
            else:
                hit = rank == lanes + (start - EDGE - SPOTS + 3 * EDGE)
            pick_ref[here, start : start + 128] = jnp.where(hit, 1.0, 0.0).astype(BF16)
    inner_pairs(images_ref, pick_ref, out_ref)


def step_parts(received_ref, damping_ref, lifted_ref):
    total = received_ref[0]
    for peer in range(1, LOAD):
        total = total + received_ref[peer]
    step = damping_ref[...] / jnp.sqrt(total[MODES : MODES + 1] / ENTRIES + EPSILON)
    correction = jnp.where(rows_of(total.shape) < MODES, total, 0.0)
    stacked = jnp.concatenate(split3(correction) + (jnp.zeros((COLS - 48, COLS), BF16),), axis=0)
    return step, dot(lifted_ref[...], stacked)


def advance(first, received_ref, damping_ref, lifted_ref, operator_ref, send_ref, residual_ref, *rest):
    step, lifted = step_parts(received_ref, damping_ref, lifted_ref)
    if first:
        iterate_ref, images_ref, down_ref, up_ref = rest
        iterate = step * (residual_ref[0] - lifted)
    else:
        before_ref, iterate_ref, images_ref, down_ref, up_ref = rest
        iterate = before_ref[...] + step * (residual_ref[...] - lifted)
    iterate_ref[...] = iterate
    images = dot(operator_ref[0], iterate.astype(BF16)).astype(BF16)
    images_ref[...] = images
    edges = dot(send_ref[...], images).astype(BF16)
    down_ref[...] = edges[:EDGE]
    up_ref[...] = edges[EDGE:]


def inner_pairs(images_ref, pick_ref, out_ref):
    out_ref[...] = dot(pick_ref[:, EDGE : EDGE + SPOTS], images_ref[...])


def inner_classes(images_ref, pick_ref, received_ref, middle_ref, out_ref, classes_ref):
    here = lax.axis_index("load")
    right = received_ref[jnp.minimum(here + 1, LOAD - 1)][13:14]
    left = received_ref[jnp.maximum(here - 1, 0)][14:15]
    right = jnp.where(here < LOAD - 1, right, 0.0)
    left = jnp.where(here > 0, left, 0.0)
    right = jnp.broadcast_to(right, (128, 128)).T[:16]
    left = jnp.broadcast_to(left, (128, 128)).T[:16]
    lanes = lanes_of((16, 128))
    classes_ref[:, :128] = middle_ref[...]
    classes_ref[:, 128:] = jnp.where(lanes == 0, right, jnp.where(lanes == 127, left, 0.0))
    inner_pairs(images_ref, pick_ref, out_ref)


def residual_terms(
    rhs_ref, images_ref, inner_ref, pick_ref, before_ref, after_ref, basis_ref, class_ref, residual_ref, out_ref
):
    partners = inner_ref[...] + dot(pick_ref[:, :EDGE], before_ref[...])
    partners = partners + dot(pick_ref[:, EDGE + SPOTS :], after_ref[...])
    residual = rhs_ref[0] - (images_ref[...].astype(F32) + partners)
    residual_ref[...] = residual
    rows = coarse_rows(basis_ref, residual)
    classes = (class_ref[...] + 1).astype(F32)
    row = rows_of(rows.shape)
    rows = jnp.where(row == 13, classes[0:1], jnp.where(row == 14, classes[7:8], rows))
    for peer in range(SUB):
        out_ref[peer] = rows


def gradients(
    received_ref,
    damping_ref,
    lifted_ref,
    residual_ref,
    iterate_ref,
    recovery_ref,
    base_ref,
    adjoint_ref,
    voxel_ref,
    multipliers_ref,
    out_ref,
):
    step, lifted = step_parts(received_ref, damping_ref, lifted_ref)
    multipliers = iterate_ref[...] + step * (residual_ref[...] - lifted)
    multipliers_ref[0] = multipliers
    displaced = base_ref[0].astype(F32) - dot(recovery_ref[0], multipliers.astype(BF16))
    products = displaced * adjoint_ref[0].astype(F32)
    first = EDOF * rows_of((128, UNKNOWNS))
    lanes = lanes_of((128, UNKNOWNS))
    groups = jnp.where((lanes >= first) & (lanes < first + EDOF), 1.0, 0.0).astype(BF16)
    sums = dot(groups, jnp.concatenate(split2(products), axis=1))
    element = jnp.sum(sums, axis=1, keepdims=True) / math.sqrt(EDOF * COLS)
    voxel = voxel_ref[...]
    column = jnp.broadcast_to(voxel & 127, (128, 128)).astype(F32).T.astype(jnp.int32)
    placed = jnp.where(column == lanes_of((128, 128)), element, 0.0)
    rows = GRID_ROWS + 16
    at_row = jnp.where(rows_of((rows, 128)) - 2 == (voxel >> 7), 1.0, 0.0).astype(BF16)
    parts = dot(at_row, jnp.concatenate(split3(placed), axis=1))
    spread = parts[:, :COLS] + parts[:, COLS : 2 * COLS] + parts[:, 2 * COLS :]
    for peer in range(SUB):
        out_ref[peer] = spread[8 * peer : 8 * peer + 16]


def smooth(middle_ref, left_ref, right_ref, classes_ref, out_ref):
    beside = jnp.where(lanes_of((16, 128)) < 64, right_ref[...], left_ref[...])
    field = jnp.concatenate([middle_ref[...], beside], axis=1)
    classes = classes_ref[...]

    def moved(value, row, lane):
        if row:
            value = pltpu.roll(value, row % 16, axis=0)
        if lane:
            value = pltpu.roll(value, lane % 256, axis=1)
        return value

    for _ in range(2):
        twice = 2.0 * field
        up, down = moved(field, 1, 0), moved(field, -1, 0)
        along_rows = down + up - twice
        along_cols = moved(field, 0, -1) + moved(field, 0, 1) - twice
        diag_main = moved(down, 0, -1) + moved(up, 0, 1) - twice
        diag_anti = moved(down, 0, 1) + moved(up, 0, -1) - twice
        chosen = jnp.where(
            classes == 1.0,
            along_rows,
            jnp.where(classes == 2.0, along_cols, jnp.where(classes == 3.0, diag_main, diag_anti)),
        )
        field = field + FIBRE_RATE * chosen + ISO_RATE * (along_rows + along_cols)
        field = jnp.where(classes > 0.0, field, 0.0)
    out_ref[...] = field[2:10, :128]


def both_ways(value, axes, size, wrap):
    up = [(i, (i + 1) % size) for i in range(size if wrap else size - 1)]
    down = [(j, i) for i, j in up]
    return lax.ppermute(value, axes, up), lax.ppermute(value, axes, down)


def on_device(
    dual_ops,
    dual_rhs,
    partner,
    coarse_basis,
    coarse_inverse,
    damping,
    recovery,
    base_disp,
    adjoint,
    elem_voxel,
    fibre_class,
):
    damping = damping.reshape(1, COLS)
    tall = ((SPOTS, COLS), F32)
    to_sub = ((SUB, 16, COLS), F32)
    to_load = ((LOAD, 16, COLS), F32)
    edge = ((EDGE, COLS), BF16)
    whole = ("sub", "load")
    up = [(i, (i + 1) % (SUB * LOAD)) for i in range(SUB * LOAD)]
    down = [(j, i) for i, j in up]

    def over(value, axis):
        return lax.all_to_all(value, axis, 0, 0, tiled=True)

    sent, send, lifted = call(
        first_terms,
        [((SUB, 24, COLS), F32), ((2 * EDGE, SPOTS), BF16), ((SPOTS, COLS), BF16)],
        (dual_rhs, coarse_basis, coarse_inverse, partner),
        "first_terms",
        scratch=[
            pltpu.VMEM(dual_rhs.shape, F32),
            pltpu.VMEM(coarse_basis.shape, BF16),
            pltpu.VMEM(coarse_inverse.shape, F32),
            pltpu.VMEM(partner.shape, jnp.int32),
        ]
        + [pltpu.SemaphoreType.DMA] * 4,
        far=(0, 1, 2, 3),
        limit=FIRST,
    )
    received = over(sent, "sub")
    partial, block, operator, residual = call(
        first_partial,
        [to_load, ((COLS, 2 * SUB * 16), BF16), (dual_ops.shape, BF16), (dual_rhs.shape, F32)],
        (received, dual_ops, dual_rhs),
        "first_partial",
        scratch=[pltpu.SemaphoreType.DMA] * 2,
        far=(1, 2),
        limit=PART,
    )
    before = ()
    for iteration in range(2):
        received = over(partial, "load")
        iterate, images, lower, upper = call(
            functools.partial(advance, iteration == 0),
            [tall, ((SPOTS, COLS), BF16), edge, edge],
            (received, damping, lifted, (operator, dual_ops)[iteration], send, residual) + before,
            "advance",
        )
        before = (iterate,)
        from_before = lax.ppermute(upper, whole, up)
        from_after = lax.ppermute(lower, whole, down)
        if iteration == 0:
            inner, pick = call(
                first_inner, [tall, ((SPOTS, SPOTS + 2 * EDGE), BF16)], (images, partner), "first_inner",
                flops=2 * SPOTS * SPOTS * 1024, moved=8 * 2**20,
            )
        else:
            inner, classes = call(
                inner_classes, [tall, ((16, 2 * COLS), F32)], (images, pick, received, middle), "inner_classes",
                flops=2 * SPOTS * SPOTS * 256, moved=4 * 2**20,
            )
        residual, sent = call(
            residual_terms,
            [tall, to_sub],
            (dual_rhs, images, inner, pick, from_before, from_after, coarse_basis, fibre_class),
            "residual_terms",
        )
        received = over(sent, "sub")
        if iteration == 0:
            partial, middle = call(
                class_partial, [to_load, ((16, COLS), F32)], (received, block, fibre_class), "class_partial"
            )
        else:
            (partial,) = call(later_partial, [to_load], (received, block), "later_partial")
    received = over(partial, "load")
    multipliers, sent = call(
        gradients,
        [((1, SPOTS, COLS), F32), to_sub],
        (received, damping, lifted, residual, iterate, recovery, base_disp, adjoint, elem_voxel),
        "gradients",
    )
    middle = jnp.sum(over(sent, "sub"), axis=0)
    left, right = both_ways(middle, "load", LOAD, False)
    (field,) = call(
        smooth,
        [(fibre_class.shape, F32)],
        (middle, left, right, classes),
        "smooth",
    )
    return multipliers, field


def solution(mesh):
    placed = (
        P(("sub", "load"), None, None),
        P(("sub", "load"), None, None),
        P(("sub", "load"), None),
        P(("sub", "load"), None, None),
        P(("sub", "load"), None),
        P(),
        P(("sub", "load"), None, None),
        P(("sub", "load"), None, None),
        P(("sub", "load"), None, None),
        P(("sub", "load"), None),
        P("sub", "load"),
    )
    return jax.shard_map(
        on_device,
        mesh=mesh,
        in_specs=placed,
        out_specs=(P(("sub", "load"), None, None), P("sub", "load")),
        check_vma=False,
    )
```

```python
import functools
import math

import jax
import jax.numpy as jnp
from jax import lax
from jax.experimental import pallas as pl
from jax.experimental.pallas import tpu as pltpu
from jax.sharding import PartitionSpec as P

EDOF = 12
MODES = 12
SUB = 32
LOAD = 8
SPOTS = 1024
COLS = 128
UNKNOWNS = 1536
EDGE = 256
MARK = 120
FIRST = 60
PART = 50
ENTRIES = SUB * LOAD * SPOTS
GRID_ROWS = 256
FIBRE_RATE = 0.3
ISO_RATE = 0.05
EPSILON = 1e-06

F32 = jnp.float32
BF16 = jnp.bfloat16


def call(kernel, outs, operands, name, flops=0, moved=16 * 2**20, limit=16, scratch=(), far=()):
    vmem, hbm = pl.BlockSpec(memory_space=pltpu.VMEM), pl.BlockSpec(memory_space=pltpu.HBM)
    return pl.pallas_call(
        kernel,
        in_specs=[hbm if place in far else vmem for place in range(len(operands))],
        out_shape=[jax.ShapeDtypeStruct(shape, dtype) for shape, dtype in outs],
        scratch_shapes=list(scratch),
        compiler_params=pltpu.CompilerParams(vmem_limit_bytes=int(limit * 2**20)),
        cost_estimate=pl.CostEstimate(flops=flops, bytes_accessed=moved, transcendentals=0),
        name=name,
    )(*operands)


def split2(value):
    high = value.astype(BF16)
    return high, (value - high.astype(F32)).astype(BF16)


def split3(value):
    high = value.astype(BF16)
    rest = value - high.astype(F32)
    middle = rest.astype(BF16)
    return high, middle, (rest - middle.astype(F32)).astype(BF16)


def dot(left, right):
    return jnp.dot(left, right, preferred_element_type=F32)


def lanes_of(shape):
    return lax.broadcasted_iota(jnp.int32, shape, 1)


def rows_of(shape):
    return lax.broadcasted_iota(jnp.int32, shape, 0)


def padded_basis(basis_ref, rows):
    basis = basis_ref[0].astype(F32)
    return jnp.concatenate([basis, jnp.zeros((rows - MODES, SPOTS), F32)], axis=0)


def coarse_rows(basis_ref, residual):
    basis = padded_basis(basis_ref, 16).astype(BF16)
    parts = dot(basis, jnp.concatenate(split3(residual), axis=1))
    terms = parts[:, :COLS] + parts[:, COLS : 2 * COLS] + parts[:, 2 * COLS :]
    squares = jnp.sum(residual * residual, axis=0, keepdims=True)
    return jnp.where(rows_of(terms.shape) == MODES, squares, terms)


def first_terms(
    rhs_hbm,
    basis_hbm,
    inverse_hbm,
    partner_hbm,
    out_ref,
    send_ref,
    lifted_ref,
    rhs_ref,
    basis_ref,
    inverse_ref,
    partner_ref,
    rhs_sem,
    basis_sem,
    inverse_sem,
    partner_sem,
):
    copies = [
        pltpu.make_async_copy(inverse_hbm, inverse_ref, inverse_sem),
        pltpu.make_async_copy(basis_hbm, basis_ref, basis_sem),
        pltpu.make_async_copy(rhs_hbm, rhs_ref, rhs_sem),
        pltpu.make_async_copy(partner_hbm, partner_ref, partner_sem),
    ]
    for copy in copies:
        copy.start()
    copies[0].wait()
    inverse = inverse_ref[...]
    inverse = jnp.concatenate([inverse, inverse[:, :128]], axis=1)
    lanes = lanes_of((8, COLS))
    lane = lanes_of((1, COLS))
    spares = []
    for peer in range(SUB):
        start = peer * LOAD * MODES
        tile, offset = start // 128, start % 128
        piece = inverse[:, 128 * tile : 128 * tile + 256]
        if offset:
            piece = pltpu.roll(piece, 256 - offset, axis=1)
        piece = piece[:, :128]
        last = piece[8:12]
        beside = jnp.concatenate([pltpu.roll(last, 96, axis=1), pltpu.roll(last, 64, axis=1)], axis=0)
        spare = pltpu.roll(last[0:1], 64, axis=1)
        for place, turn in ((1, 96), (2, 0), (3, 32)):
            part = last[place : place + 1]
            spare = jnp.where(lane < 32 * place, spare, pltpu.roll(part, turn, axis=1) if turn else part)
        out_ref[peer, 16:, :] = jnp.where(lanes < 96, piece[:8], beside)
        spares.append(spare)
    copies[3].wait()
    edge_rows(partner_ref[...].astype(F32), send_ref)
    copies[1].wait()
    basis = padded_basis(basis_ref, COLS).T
    basis = basis + pltpu.roll(basis, 16, axis=1) + pltpu.roll(basis, 32, axis=1)
    lifted_ref[...] = basis.astype(BF16)
    copies[2].wait()
    rows = coarse_rows(basis_ref, rhs_ref[0])
    row = rows_of(rows.shape)
    for peer in range(SUB):
        out_ref[peer, :16, :] = jnp.where(row == 15, spares[peer], rows)


def partial_rows(high, low, terms, out_ref):
    terms_high, terms_low = split2(terms)
    partial = dot(high, terms_high) + dot(high, terms_low) + dot(low, terms_high)
    last = jnp.concatenate([partial[MARK : MARK + 1], jnp.zeros((3, COLS), F32)], axis=0)
    for peer in range(LOAD):
        out_ref[peer] = jnp.concatenate([partial[MODES * peer : MODES * peer + MODES], last], axis=0)


def first_partial(
    received_ref, operator_hbm, out_ref, block_ref, operator_ref, operator_sem
):
    copy = pltpu.make_async_copy(operator_hbm, operator_ref, operator_sem)
    copy.start()
    terms = received_ref[:, :16, :].reshape(SUB * 16, COLS)
    packed = received_ref[:, 16:, :].reshape(SUB * 8, COLS)
    lanes = lanes_of((SUB * 8, COLS))
    upper = jnp.where(lanes < 96, packed, 0.0).reshape(SUB, 8, COLS)
    first = pltpu.roll(packed, 32, axis=1).reshape(SUB, 8, COLS)[:, :4]
    second = pltpu.roll(packed, 64, axis=1).reshape(SUB, 8, COLS)[:, 4:]
    spare = received_ref[:, 15, :]
    third = [pltpu.roll(spare, 64, axis=1), pltpu.roll(spare, 32, axis=1), spare, pltpu.roll(spare, 96, axis=1)]
    third = jnp.concatenate([part.reshape(SUB, 1, COLS) for part in third], axis=1)
    lanes = lax.broadcasted_iota(jnp.int32, (SUB, 4, COLS), 2)
    lower = jnp.where(lanes < 32, first, jnp.where(lanes < 64, second, jnp.where(lanes < 96, third, 0.0)))
    places = lax.broadcasted_iota(jnp.int32, (SUB, 4, COLS), 1)
    mark = jnp.where((places == 0) & (lanes == MARK), 1.0, 0.0)
    block = jnp.concatenate([upper, jnp.concatenate([lower, mark], axis=1)], axis=1)
    high, low = split2(block.reshape(SUB * 16, COLS).T)
    block_ref[:, : SUB * 16] = high
    block_ref[:, SUB * 16 :] = low
    partial_rows(high, low, terms, out_ref)
    copy.wait()


def later_partial(received_ref, block_ref, out_ref):
    terms = received_ref[...].reshape(SUB * 16, COLS)
    partial_rows(block_ref[:, : SUB * 16], block_ref[:, SUB * 16 :], terms, out_ref)


def class_partial(received_ref, block_ref, class_ref, out_ref, middle_ref):
    later_partial(received_ref, block_ref, out_ref)
    here = lax.axis_index("sub")
    above = received_ref[jnp.maximum(here - 1, 0)][14:15]
    below = received_ref[jnp.minimum(here + 1, SUB - 1)][13:14]
    above = jnp.where(here > 0, above, 0.0)
    below = jnp.where(here < SUB - 1, below, 0.0)
    classes = (class_ref[...] + 1).astype(F32)
    gap = jnp.zeros((1, COLS), F32)
    middle = jnp.concatenate([gap, above, classes, below, gap, gap, gap, gap, gap], axis=0)
    middle_ref[...] = middle
    sides = jnp.concatenate([middle, jnp.zeros((COLS - 16, COLS), F32)], axis=0).T
    for peer in range(LOAD):
        out_ref[peer, 13:14, :] = sides[0:1]
        out_ref[peer, 14:15, :] = sides[127:128]


def edge_rows(partners, send_ref):
    to_before = jnp.where(partners < SPOTS, 1.0, 0.0)
    to_after = jnp.where(partners >= 2 * SPOTS, 1.0, 0.0)
    sides = jnp.concatenate([to_before, to_after, jnp.zeros((6, SPOTS), F32)], axis=0)
    lanes = lanes_of(sides.shape)
    place = sides
    for power in range(10):
        earlier = pltpu.roll(place, 1 << power, axis=1)
        place = place + jnp.where(lanes >= 1 << power, earlier, 0.0)
    place = jnp.where(sides > 0.0, place - 1.0, -1.0)
    slots = rows_of((EDGE, SPOTS)).astype(F32)
    send_ref[:EDGE, :] = jnp.where(slots == place[0:1], 1.0, 0.0).astype(BF16)
    send_ref[EDGE:, :] = jnp.where(slots == place[1:2], 1.0, 0.0).astype(BF16)


def first_inner(images_ref, partner_ref, out_ref, pick_ref):
    partners = partner_ref[...].astype(F32)
    lanes = lanes_of((128, 128)).astype(F32)
    for block in range(SPOTS // 128):
        here = slice(128 * block, 128 * block + 128)
        wanted = jnp.broadcast_to(partners[:, here], (128, 128)).T
        smaller = jnp.zeros((128, 128), F32)
        for tile in range(SPOTS // 128):
            smaller = smaller + jnp.where(partners[:, 128 * tile : 128 * tile + 128] < wanted, 1.0, 0.0)
        rank = jnp.broadcast_to(jnp.sum(smaller, axis=1, keepdims=True), (128, 128))
        for tile in range((2 * EDGE + SPOTS) // 128):
            start = 128 * tile
            if start < EDGE:
                hit = rank == lanes + start
            elif start < EDGE + SPOTS:
                hit = wanted == lanes + (start - EDGE + SPOTS)
            else:
                hit = rank == lanes + (start - EDGE - SPOTS + 3 * EDGE)
            pick_ref[here, start : start + 128] = jnp.where(hit, 1.0, 0.0).astype(BF16)
    inner_pairs(images_ref, pick_ref, out_ref)


def step_parts(received_ref, damping_ref, lifted_ref):
    total = received_ref[0]
    for peer in range(1, LOAD):
        total = total + received_ref[peer]
    step = damping_ref[...] / jnp.sqrt(total[MODES : MODES + 1] / ENTRIES + EPSILON)
    correction = jnp.where(rows_of(total.shape) < MODES, total, 0.0)
    stacked = jnp.concatenate(split3(correction) + (jnp.zeros((COLS - 48, COLS), BF16),), axis=0)
    return step, dot(lifted_ref[...], stacked)


def advance(first, received_ref, damping_ref, lifted_ref, operator_ref, send_ref, residual_ref, *rest):
    step, lifted = step_parts(received_ref, damping_ref, lifted_ref)
    if first:
        iterate_ref, images_ref, down_ref, up_ref = rest
        iterate = step * (residual_ref[0] - lifted)
    else:
        before_ref, iterate_ref, images_ref, down_ref, up_ref = rest
        iterate = before_ref[...] + step * (residual_ref[...] - lifted)
    iterate_ref[...] = iterate
    images = dot(operator_ref[0], iterate.astype(BF16)).astype(BF16)
    images_ref[...] = images
    edges = dot(send_ref[...], images).astype(BF16)
    down_ref[...] = edges[:EDGE]
    up_ref[...] = edges[EDGE:]


def inner_pairs(images_ref, pick_ref, out_ref):
    out_ref[...] = dot(pick_ref[:, EDGE : EDGE + SPOTS], images_ref[...])


def inner_classes(images_ref, pick_ref, received_ref, middle_ref, out_ref, classes_ref):
    here = lax.axis_index("load")
    right = received_ref[jnp.minimum(here + 1, LOAD - 1)][13:14]
    left = received_ref[jnp.maximum(here - 1, 0)][14:15]
    right = jnp.where(here < LOAD - 1, right, 0.0)
    left = jnp.where(here > 0, left, 0.0)
    right = jnp.broadcast_to(right, (128, 128)).T[:16]
    left = jnp.broadcast_to(left, (128, 128)).T[:16]
    lanes = lanes_of((16, 128))
    classes_ref[:, :128] = middle_ref[...]
    classes_ref[:, 128:] = jnp.where(lanes == 0, right, jnp.where(lanes == 127, left, 0.0))
    inner_pairs(images_ref, pick_ref, out_ref)


def residual_terms(
    rhs_ref, images_ref, inner_ref, pick_ref, before_ref, after_ref, basis_ref, class_ref, residual_ref, out_ref
):
    partners = inner_ref[...] + dot(pick_ref[:, :EDGE], before_ref[...])
    partners = partners + dot(pick_ref[:, EDGE + SPOTS :], after_ref[...])
    residual = rhs_ref[0] - (images_ref[...].astype(F32) + partners)
    residual_ref[...] = residual
    rows = coarse_rows(basis_ref, residual)
    classes = (class_ref[...] + 1).astype(F32)
    row = rows_of(rows.shape)
    rows = jnp.where(row == 13, classes[0:1], jnp.where(row == 14, classes[7:8], rows))
    for peer in range(SUB):
        out_ref[peer] = rows


def gradients(
    received_ref,
    damping_ref,
    lifted_ref,
    residual_ref,
    iterate_ref,
    recovery_ref,
    base_ref,
    adjoint_ref,
    voxel_ref,
    multipliers_ref,
    out_ref,
):
    step, lifted = step_parts(received_ref, damping_ref, lifted_ref)
    multipliers = iterate_ref[...] + step * (residual_ref[...] - lifted)
    multipliers_ref[0] = multipliers
    displaced = base_ref[0].astype(F32) - dot(recovery_ref[0], multipliers.astype(BF16))
    products = displaced * adjoint_ref[0].astype(F32)
    first = EDOF * rows_of((128, UNKNOWNS))
    lanes = lanes_of((128, UNKNOWNS))
    groups = jnp.where((lanes >= first) & (lanes < first + EDOF), 1.0, 0.0).astype(BF16)
    sums = dot(groups, jnp.concatenate(split2(products), axis=1))
    element = jnp.sum(sums, axis=1, keepdims=True) / math.sqrt(EDOF * COLS)
    voxel = voxel_ref[...]
    column = jnp.broadcast_to(voxel & 127, (128, 128)).astype(F32).T.astype(jnp.int32)
    placed = jnp.where(column == lanes_of((128, 128)), element, 0.0)
    rows = GRID_ROWS + 16
    at_row = jnp.where(rows_of((rows, 128)) - 2 == (voxel >> 7), 1.0, 0.0).astype(BF16)
    parts = dot(at_row, jnp.concatenate(split3(placed), axis=1))
    spread = parts[:, :COLS] + parts[:, COLS : 2 * COLS] + parts[:, 2 * COLS :]
    for peer in range(SUB):
        out_ref[peer] = spread[8 * peer : 8 * peer + 16]


def smooth(middle_ref, left_ref, right_ref, classes_ref, out_ref):
    beside = jnp.where(lanes_of((16, 128)) < 64, right_ref[...], left_ref[...])
    field = jnp.concatenate([middle_ref[...], beside], axis=1)
    classes = classes_ref[...]

    def moved(value, row, lane):
        if row:
            value = pltpu.roll(value, row % 16, axis=0)
        if lane:
            value = pltpu.roll(value, lane % 256, axis=1)
        return value

    for _ in range(2):
        twice = 2.0 * field
        up, down = moved(field, 1, 0), moved(field, -1, 0)
        along_rows = down + up - twice
        along_cols = moved(field, 0, -1) + moved(field, 0, 1) - twice
        diag_main = moved(down, 0, -1) + moved(up, 0, 1) - twice
        diag_anti = moved(down, 0, 1) + moved(up, 0, -1) - twice
        chosen = jnp.where(
            classes == 1.0,
            along_rows,
            jnp.where(classes == 2.0, along_cols, jnp.where(classes == 3.0, diag_main, diag_anti)),
        )
        field = field + FIBRE_RATE * chosen + ISO_RATE * (along_rows + along_cols)
        field = jnp.where(classes > 0.0, field, 0.0)
    out_ref[...] = field[2:10, :128]


def both_ways(value, axes, size, wrap):
    up = [(i, (i + 1) % size) for i in range(size if wrap else size - 1)]
    down = [(j, i) for i, j in up]
    return lax.ppermute(value, axes, up), lax.ppermute(value, axes, down)


def on_device(
    dual_ops,
    dual_rhs,
    partner,
    coarse_basis,
    coarse_inverse,
    damping,
    recovery,
    base_disp,
    adjoint,
    elem_voxel,
    fibre_class,
):
    damping = damping.reshape(1, COLS)
    tall = ((SPOTS, COLS), F32)
    to_sub = ((SUB, 16, COLS), F32)
    to_load = ((LOAD, 16, COLS), F32)
    edge = ((EDGE, COLS), BF16)
    whole = ("sub", "load")
    up = [(i, (i + 1) % (SUB * LOAD)) for i in range(SUB * LOAD)]
    down = [(j, i) for i, j in up]

    def over(value, axis):
        return lax.all_to_all(value, axis, 0, 0, tiled=True)

    sent, send, lifted = call(
        first_terms,
        [((SUB, 24, COLS), F32), ((2 * EDGE, SPOTS), BF16), ((SPOTS, COLS), BF16)],
        (dual_rhs, coarse_basis, coarse_inverse, partner),
        "first_terms",
        scratch=[
            pltpu.VMEM(dual_rhs.shape, F32),
            pltpu.VMEM(coarse_basis.shape, BF16),
            pltpu.VMEM(coarse_inverse.shape, F32),
            pltpu.VMEM(partner.shape, jnp.int32),
        ]
        + [pltpu.SemaphoreType.DMA] * 4,
        far=(0, 1, 2, 3),
        limit=FIRST,
    )
    received = over(sent, "sub")
    partial, block, operator = call(
        first_partial,
        [to_load, ((COLS, 2 * SUB * 16), BF16), (dual_ops.shape, BF16)],
        (received, dual_ops),
        "first_partial",
        scratch=[pltpu.SemaphoreType.DMA],
        far=(1,),
        limit=PART,
    )
    residual = dual_rhs
    before = ()
    for iteration in range(2):
        received = over(partial, "load")
        iterate, images, lower, upper = call(
            functools.partial(advance, iteration == 0),
            [tall, ((SPOTS, COLS), BF16), edge, edge],
            (received, damping, lifted, (operator, dual_ops)[iteration], send, residual) + before,
            "advance",
        )
        before = (iterate,)
        from_before = lax.ppermute(upper, whole, up)
        from_after = lax.ppermute(lower, whole, down)
        if iteration == 0:
            inner, pick = call(
                first_inner, [tall, ((SPOTS, SPOTS + 2 * EDGE), BF16)], (images, partner), "first_inner",
                flops=2 * SPOTS * SPOTS * 1024, moved=8 * 2**20,
            )
        else:
            inner, classes = call(
                inner_classes, [tall, ((16, 2 * COLS), F32)], (images, pick, received, middle), "inner_classes",
                flops=2 * SPOTS * SPOTS * 256, moved=4 * 2**20,
            )
        residual, sent = call(
            residual_terms,
            [tall, to_sub],
            (dual_rhs, images, inner, pick, from_before, from_after, coarse_basis, fibre_class),
            "residual_terms",
        )
        received = over(sent, "sub")
        if iteration == 0:
            partial, middle = call(
                class_partial, [to_load, ((16, COLS), F32)], (received, block, fibre_class), "class_partial"
            )
        else:
            (partial,) = call(later_partial, [to_load], (received, block), "later_partial")
    received = over(partial, "load")
    multipliers, sent = call(
        gradients,
        [((1, SPOTS, COLS), F32), to_sub],
        (received, damping, lifted, residual, iterate, recovery, base_disp, adjoint, elem_voxel),
        "gradients",
    )
    middle = jnp.sum(over(sent, "sub"), axis=0)
    left, right = both_ways(middle, "load", LOAD, False)
    (field,) = call(
        smooth,
        [(fibre_class.shape, F32)],
        (middle, left, right, classes),
        "smooth",
    )
    return multipliers, field


def solution(mesh):
    placed = (
        P(("sub", "load"), None, None),
        P(("sub", "load"), None, None),
        P(("sub", "load"), None),
        P(("sub", "load"), None, None),
        P(("sub", "load"), None),
        P(),
        P(("sub", "load"), None, None),
        P(("sub", "load"), None, None),
        P(("sub", "load"), None, None),
        P(("sub", "load"), None),
        P("sub", "load"),
    )
    return jax.shard_map(
        on_device,
        mesh=mesh,
        in_specs=placed,
        out_specs=(P(("sub", "load"), None, None), P("sub", "load")),
        check_vma=False,
    )
```

```python
import functools
import math

import jax
import jax.numpy as jnp
from jax import lax
from jax.experimental import pallas as pl
from jax.experimental.pallas import tpu as pltpu
from jax.sharding import PartitionSpec as P

EDOF = 12
MODES = 12
SUB = 32
LOAD = 8
SPOTS = 1024
COLS = 128
UNKNOWNS = 1536
EDGE = 256
FIRST = 60
PART = 50
ENTRIES = SUB * LOAD * SPOTS
GRID_ROWS = 256
FIBRE_RATE = 0.3
ISO_RATE = 0.05
EPSILON = 1e-06

F32 = jnp.float32
BF16 = jnp.bfloat16


def call(kernel, outs, operands, name, flops=0, moved=16 * 2**20, limit=16, scratch=(), far=(), far_out=()):
    vmem, hbm = pl.BlockSpec(memory_space=pltpu.VMEM), pl.BlockSpec(memory_space=pltpu.HBM)
    return pl.pallas_call(
        kernel,
        in_specs=[hbm if place in far else vmem for place in range(len(operands))],
        out_specs=[hbm if place in far_out else vmem for place in range(len(outs))],
        out_shape=[jax.ShapeDtypeStruct(shape, dtype) for shape, dtype in outs],
        scratch_shapes=list(scratch),
        compiler_params=pltpu.CompilerParams(vmem_limit_bytes=int(limit * 2**20)),
        cost_estimate=pl.CostEstimate(flops=flops, bytes_accessed=moved, transcendentals=0),
        name=name,
    )(*operands)


def split2(value):
    high = value.astype(BF16)
    return high, (value - high.astype(F32)).astype(BF16)


def split3(value):
    high = value.astype(BF16)
    rest = value - high.astype(F32)
    middle = rest.astype(BF16)
    return high, middle, (rest - middle.astype(F32)).astype(BF16)


def dot(left, right):
    return jnp.dot(left, right, preferred_element_type=F32)


def lanes_of(shape):
    return lax.broadcasted_iota(jnp.int32, shape, 1)


def rows_of(shape):
    return lax.broadcasted_iota(jnp.int32, shape, 0)


def padded_basis(basis_ref, rows):
    basis = basis_ref[0].astype(F32)
    return jnp.concatenate([basis, jnp.zeros((rows - MODES, SPOTS), F32)], axis=0)


def coarse_rows(basis_ref, residual):
    basis = padded_basis(basis_ref, 16).astype(BF16)
    parts = dot(basis, jnp.concatenate(split3(residual), axis=1))
    terms = parts[:, :COLS] + parts[:, COLS : 2 * COLS] + parts[:, 2 * COLS :]
    squares = jnp.sum(residual * residual, axis=0, keepdims=True)
    return jnp.where(rows_of(terms.shape) == MODES, squares, terms)


def first_terms(
    rhs_hbm,
    basis_hbm,
    inverse_hbm,
    partner_hbm,
    out_ref,
    send_ref,
    lifted_ref,
    rhs_ref,
    basis_ref,
    inverse_ref,
    partner_ref,
    rhs_sem,
    basis_sem,
    inverse_sem,
    partner_sem,
):
    copies = [
        pltpu.make_async_copy(inverse_hbm, inverse_ref, inverse_sem),
        pltpu.make_async_copy(basis_hbm, basis_ref, basis_sem),
        pltpu.make_async_copy(rhs_hbm, rhs_ref, rhs_sem),
        pltpu.make_async_copy(partner_hbm, partner_ref, partner_sem),
    ]
    for copy in copies:
        copy.start()
    copies[0].wait()
    inverse = inverse_ref[...]
    inverse = jnp.concatenate([inverse, inverse[:, :128]], axis=1)
    pieces = []
    for group in range(SUB):
        start = group * LOAD * MODES
        tile, offset = start // 128, start % 128
        piece = inverse[:, 128 * tile : 128 * tile + 256]
        if offset:
            piece = pltpu.roll(piece, 256 - offset, axis=1)
        pieces.append(piece[:, :128])
    lanes = lanes_of((MODES, COLS))
    masks = [(lanes >= 16 * slot) & (lanes < 16 * slot + MODES) for slot in range(8)]
    for peer in range(LOAD):
        tiles = []
        for tile in range(4):
            chosen = jnp.zeros((MODES, COLS), F32)
            for slot in range(8):
                turn = (16 * slot - MODES * peer) % 128
                piece = pieces[8 * tile + slot]
                piece = pltpu.roll(piece, turn, axis=1) if turn else piece
                chosen = jnp.where(masks[slot], piece, chosen)
            tiles.append(chosen)
        out_ref[peer, 16:, :] = jnp.concatenate(tiles, axis=0)
    copies[3].wait()
    edge_rows(partner_ref[...].astype(F32), send_ref)
    copies[1].wait()
    basis = padded_basis(basis_ref, COLS).T
    basis = basis + pltpu.roll(basis, 16, axis=1) + pltpu.roll(basis, 32, axis=1)
    lifted_ref[...] = basis.astype(BF16)
    copies[2].wait()
    rows = coarse_rows(basis_ref, rhs_ref[0])
    for peer in range(LOAD):
        out_ref[peer, :16, :] = rows


def partial_rows(high, low, terms, out_ref):
    terms_high, terms_low = split2(terms)
    partial = dot(high, terms_high) + dot(high, terms_low) + dot(low, terms_high)
    out_ref[...] = partial.reshape(SUB, 16, COLS)


def first_partial(received_ref, operator_hbm, out_ref, block_ref, operator_ref, operator_sem):
    copy = pltpu.make_async_copy(operator_hbm, operator_ref, operator_sem)
    copy.start()
    terms = received_ref[:, :16, :].reshape(LOAD * 16, COLS)
    lanes = lax.broadcasted_iota(jnp.int32, (LOAD, 4, COLS), 2)
    places = lax.broadcasted_iota(jnp.int32, (LOAD, 4, COLS), 1)
    mark = jnp.where((places == 0) & (lanes % 16 == MODES), 1.0, 0.0)
    blocks = []
    for tile in range(4):
        start = 16 + MODES * tile
        rows = jnp.concatenate([received_ref[:, start : start + MODES, :], mark], axis=1)
        blocks.append(rows.reshape(LOAD * 16, COLS).T)
    high, low = split2(jnp.concatenate(blocks, axis=0))
    block_ref[:, :COLS] = high
    block_ref[:, COLS:] = low
    partial_rows(high, low, terms, out_ref)
    copy.wait()


def later_partial(received_ref, block_ref, out_ref):
    terms = received_ref[...].reshape(LOAD * 16, COLS)
    partial_rows(block_ref[:, :COLS], block_ref[:, COLS:], terms, out_ref)


def class_partial(received_ref, block_ref, class_ref, out_ref, sides_ref):
    later_partial(received_ref, block_ref, out_ref)
    here = lax.axis_index("load")
    right = received_ref[jnp.minimum(here + 1, LOAD - 1)][13:14]
    left = received_ref[jnp.maximum(here - 1, 0)][14:15]
    right = jnp.where(here < LOAD - 1, right, 0.0)
    left = jnp.where(here > 0, left, 0.0)
    lanes = lanes_of((1, COLS))
    sides = jnp.where(lanes < 8, right, jnp.where(lanes < 16, pltpu.roll(left, 8, axis=1), 0.0))
    classes = (class_ref[...] + 1).astype(F32)
    edges = jnp.concatenate([classes[0:1], classes[7:8], sides], axis=0)
    for peer in range(SUB):
        out_ref[peer, 13:16, :] = edges
    sides_ref[...] = jnp.broadcast_to(sides, sides_ref.shape)


def edge_rows(partners, send_ref):
    to_before = jnp.where(partners < SPOTS, 1.0, 0.0)
    to_after = jnp.where(partners >= 2 * SPOTS, 1.0, 0.0)
    sides = jnp.concatenate([to_before, to_after, jnp.zeros((6, SPOTS), F32)], axis=0)
    lanes = lanes_of(sides.shape)
    place = sides
    for power in range(10):
        earlier = pltpu.roll(place, 1 << power, axis=1)
        place = place + jnp.where(lanes >= 1 << power, earlier, 0.0)
    place = jnp.where(sides > 0.0, place - 1.0, -1.0)
    slots = rows_of((EDGE, SPOTS)).astype(F32)
    send_ref[:EDGE, :] = jnp.where(slots == place[0:1], 1.0, 0.0).astype(BF16)
    send_ref[EDGE:, :] = jnp.where(slots == place[1:2], 1.0, 0.0).astype(BF16)


def first_inner(images_ref, partner_ref, out_ref, pick_ref):
    partners = partner_ref[...].astype(F32)
    lanes = lanes_of((128, 128)).astype(F32)
    for block in range(SPOTS // 128):
        here = slice(128 * block, 128 * block + 128)
        wanted = jnp.broadcast_to(partners[:, here], (128, 128)).T
        smaller = jnp.zeros((128, 128), F32)
        for tile in range(SPOTS // 128):
            smaller = smaller + jnp.where(partners[:, 128 * tile : 128 * tile + 128] < wanted, 1.0, 0.0)
        rank = jnp.broadcast_to(jnp.sum(smaller, axis=1, keepdims=True), (128, 128))
        for tile in range((2 * EDGE + SPOTS) // 128):
            start = 128 * tile
            if start < EDGE:
                hit = rank == lanes + start
            elif start < EDGE + SPOTS:
                hit = wanted == lanes + (start - EDGE + SPOTS)
            else:
                hit = rank == lanes + (start - EDGE - SPOTS + 3 * EDGE)
            pick_ref[here, start : start + 128] = jnp.where(hit, 1.0, 0.0).astype(BF16)
    inner_pairs(images_ref, pick_ref, out_ref)


def step_parts(received_ref, damping_ref, lifted_ref):
    total = jnp.sum(received_ref[...], axis=0)
    step = damping_ref[...] / jnp.sqrt(total[MODES : MODES + 1] / ENTRIES + EPSILON)
    correction = jnp.where(rows_of(total.shape) < MODES, total, 0.0)
    stacked = jnp.concatenate(split3(correction) + (jnp.zeros((COLS - 48, COLS), BF16),), axis=0)
    return step, dot(lifted_ref[...], stacked)


def advance(first, received_ref, damping_ref, lifted_ref, operator_ref, send_ref, residual_ref, *rest):
    step, lifted = step_parts(received_ref, damping_ref, lifted_ref)
    if first:
        iterate_ref, images_ref, down_ref, up_ref = rest
        iterate = step * (residual_ref[0] - lifted)
    else:
        before_ref, iterate_ref, images_ref, down_ref, up_ref = rest
        iterate = before_ref[...] + step * (residual_ref[...] - lifted)
    iterate_ref[...] = iterate
    images = dot(operator_ref[0], iterate.astype(BF16)).astype(BF16)
    images_ref[...] = images
    edges = dot(send_ref[...], images).astype(BF16)
    down_ref[...] = edges[:EDGE]
    up_ref[...] = edges[EDGE:]


def inner_pairs(images_ref, pick_ref, out_ref):
    out_ref[...] = dot(pick_ref[:, EDGE : EDGE + SPOTS], images_ref[...])


def inner_classes(images_ref, pick_ref, received_ref, class_ref, sides_ref, out_ref, classes_ref):
    here = lax.axis_index("sub")
    above = jnp.where(here > 0, received_ref[jnp.maximum(here - 1, 0)], 0.0)
    below = jnp.where(here < SUB - 1, received_ref[jnp.minimum(here + 1, SUB - 1)], 0.0)
    classes = (class_ref[...] + 1).astype(F32)
    gap = jnp.zeros((1, COLS), F32)
    middle = jnp.concatenate([gap, above[14:15], classes, below[13:14], gap, gap, gap, gap, gap], axis=0)
    lanes = lanes_of((1, COLS))

    def column(offset):
        def at(value, source, target):
            turn = (target - source - offset) % 128
            return pltpu.roll(value, turn, axis=1) if turn else value

        own = at(sides_ref[0:1], 0, 2)
        own = jnp.where((lanes >= 2) & (lanes < 10), own, 0.0)
        own = jnp.where(lanes == 1, at(above[15:16], 7, 1), own)
        own = jnp.where(lanes == 10, at(below[15:16], 0, 10), own)
        return jnp.broadcast_to(own, (128, 128)).T[:16]

    right, left = column(0), column(8)
    wide = lanes_of((16, 128))
    classes_ref[:, :128] = middle
    classes_ref[:, 128:] = jnp.where(wide == 0, right, jnp.where(wide == 127, left, 0.0))
    inner_pairs(images_ref, pick_ref, out_ref)


def residual_terms(
    rhs_ref, images_ref, inner_ref, pick_ref, before_ref, after_ref, basis_ref, class_ref, residual_ref, out_ref
):
    partners = inner_ref[...] + dot(pick_ref[:, :EDGE], before_ref[...])
    partners = partners + dot(pick_ref[:, EDGE + SPOTS :], after_ref[...])
    residual = rhs_ref[0] - (images_ref[...].astype(F32) + partners)
    residual_ref[...] = residual
    rows = coarse_rows(basis_ref, residual)
    classes = (class_ref[...] + 1).astype(F32)
    row = rows_of(rows.shape)
    columns = jnp.concatenate([classes, jnp.zeros((COLS - 8, COLS), F32)], axis=0).T
    rows = jnp.where(row == 13, columns[0:1], jnp.where(row == 14, columns[127:128], rows))
    for peer in range(LOAD):
        out_ref[peer] = rows


def gradients(
    received_ref,
    damping_ref,
    lifted_ref,
    residual_ref,
    iterate_ref,
    recovery_ref,
    base_ref,
    adjoint_ref,
    voxel_ref,
    multipliers_hbm,
    out_ref,
    multipliers_ref,
    multipliers_sem,
):
    step, lifted = step_parts(received_ref, damping_ref, lifted_ref)
    multipliers = iterate_ref[...] + step * (residual_ref[...] - lifted)
    multipliers_ref[0] = multipliers
    copy = pltpu.make_async_copy(multipliers_ref, multipliers_hbm, multipliers_sem)
    copy.start()
    displaced = base_ref[0].astype(F32) - dot(recovery_ref[0], multipliers.astype(BF16))
    products = displaced * adjoint_ref[0].astype(F32)
    first = EDOF * rows_of((128, UNKNOWNS))
    lanes = lanes_of((128, UNKNOWNS))
    groups = jnp.where((lanes >= first) & (lanes < first + EDOF), 1.0, 0.0).astype(BF16)
    sums = dot(groups, jnp.concatenate(split2(products), axis=1))
    element = jnp.sum(sums, axis=1, keepdims=True) / math.sqrt(EDOF * COLS)
    voxel = voxel_ref[...]
    column = jnp.broadcast_to(voxel & 127, (128, 128)).astype(F32).T.astype(jnp.int32)
    placed = jnp.where(column == lanes_of((128, 128)), element, 0.0)
    rows = GRID_ROWS + 16
    at_row = jnp.where(rows_of((rows, 128)) - 2 == (voxel >> 7), 1.0, 0.0).astype(BF16)
    parts = dot(at_row, jnp.concatenate(split3(placed), axis=1))
    spread = parts[:, :COLS] + parts[:, COLS : 2 * COLS] + parts[:, 2 * COLS :]
    for peer in range(SUB):
        out_ref[peer] = spread[8 * peer : 8 * peer + 16]
    copy.wait()


def smooth(middle_ref, left_ref, right_ref, classes_ref, out_ref):
    beside = jnp.where(lanes_of((16, 128)) < 64, right_ref[...], left_ref[...])
    field = jnp.concatenate([middle_ref[...], beside], axis=1)
    classes = classes_ref[...]

    def moved(value, row, lane):
        if row:
            value = pltpu.roll(value, row % 16, axis=0)
        if lane:
            value = pltpu.roll(value, lane % 256, axis=1)
        return value

    for _ in range(2):
        twice = 2.0 * field
        up, down = moved(field, 1, 0), moved(field, -1, 0)
        along_rows = down + up - twice
        along_cols = moved(field, 0, -1) + moved(field, 0, 1) - twice
        diag_main = moved(down, 0, -1) + moved(up, 0, 1) - twice
        diag_anti = moved(down, 0, 1) + moved(up, 0, -1) - twice
        chosen = jnp.where(
            classes == 1.0,
            along_rows,
            jnp.where(classes == 2.0, along_cols, jnp.where(classes == 3.0, diag_main, diag_anti)),
        )
        field = field + FIBRE_RATE * chosen + ISO_RATE * (along_rows + along_cols)
        field = jnp.where(classes > 0.0, field, 0.0)
    out_ref[...] = field[2:10, :128]


def both_ways(value, axes, size, wrap):
    up = [(i, (i + 1) % size) for i in range(size if wrap else size - 1)]
    down = [(j, i) for i, j in up]
    return lax.ppermute(value, axes, up), lax.ppermute(value, axes, down)


def on_device(
    dual_ops,
    dual_rhs,
    partner,
    coarse_basis,
    coarse_inverse,
    damping,
    recovery,
    base_disp,
    adjoint,
    elem_voxel,
    fibre_class,
):
    damping = damping.reshape(1, COLS)
    tall = ((SPOTS, COLS), F32)
    to_sub = ((SUB, 16, COLS), F32)
    to_load = ((LOAD, 16, COLS), F32)
    edge = ((EDGE, COLS), BF16)
    whole = ("sub", "load")
    up = [(i, (i + 1) % (SUB * LOAD)) for i in range(SUB * LOAD)]
    down = [(j, i) for i, j in up]

    def over(value, axis):
        return lax.all_to_all(value, axis, 0, 0, tiled=True)

    sent, send, lifted = call(
        first_terms,
        [((LOAD, 64, COLS), F32), ((2 * EDGE, SPOTS), BF16), ((SPOTS, COLS), BF16)],
        (dual_rhs, coarse_basis, coarse_inverse, partner),
        "first_terms",
        scratch=[
            pltpu.VMEM(dual_rhs.shape, F32),
            pltpu.VMEM(coarse_basis.shape, BF16),
            pltpu.VMEM(coarse_inverse.shape, F32),
            pltpu.VMEM(partner.shape, jnp.int32),
        ]
        + [pltpu.SemaphoreType.DMA] * 4,
        far=(0, 1, 2, 3),
        limit=FIRST,
    )
    received = over(sent, "load")
    partial, block, operator = call(
        first_partial,
        [to_sub, ((SUB * 16, 2 * COLS), BF16), (dual_ops.shape, BF16)],
        (received, dual_ops),
        "first_partial",
        scratch=[pltpu.SemaphoreType.DMA],
        far=(1,),
        limit=PART,
    )
    residual = dual_rhs
    before = ()
    for iteration in range(2):
        received = over(partial, "sub")
        iterate, images, lower, upper = call(
            functools.partial(advance, iteration == 0),
            [tall, ((SPOTS, COLS), BF16), edge, edge],
            (received, damping, lifted, (operator, dual_ops)[iteration], send, residual) + before,
            "advance",
        )
        before = (iterate,)
        from_before = lax.ppermute(upper, whole, up)
        from_after = lax.ppermute(lower, whole, down)
        if iteration == 0:
            inner, pick = call(
                first_inner, [tall, ((SPOTS, SPOTS + 2 * EDGE), BF16)], (images, partner), "first_inner",
                flops=2 * SPOTS * SPOTS * 1024, moved=8 * 2**20,
            )
        else:
            inner, classes = call(
                inner_classes, [tall, ((16, 2 * COLS), F32)], (images, pick, received, fibre_class, sides), "inner_classes",
                flops=2 * SPOTS * SPOTS * 256, moved=4 * 2**20,
            )
        residual, sent = call(
            residual_terms,
            [tall, to_load],
            (dual_rhs, images, inner, pick, from_before, from_after, coarse_basis, fibre_class),
            "residual_terms",
        )
        received = over(sent, "load")
        if iteration == 0:
            partial, sides = call(
                class_partial, [to_sub, ((8, COLS), F32)], (received, block, fibre_class), "class_partial"
            )
        else:
            (partial,) = call(later_partial, [to_sub], (received, block), "later_partial")
    received = over(partial, "sub")
    multipliers, sent = call(
        gradients,
        [((1, SPOTS, COLS), F32), to_sub],
        (received, damping, lifted, residual, iterate, recovery, base_disp, adjoint, elem_voxel),
        "gradients",
        scratch=[pltpu.VMEM((1, SPOTS, COLS), F32), pltpu.SemaphoreType.DMA],
        far_out=(0,),
    )
    middle = jnp.sum(over(sent, "sub"), axis=0)
    left, right = both_ways(middle, "load", LOAD, False)
    (field,) = call(
        smooth,
        [(fibre_class.shape, F32)],
        (middle, left, right, classes),
        "smooth",
    )
    return multipliers, field


def solution(mesh):
    placed = (
        P(("sub", "load"), None, None),
        P(("sub", "load"), None, None),
        P(("sub", "load"), None),
        P(("sub", "load"), None, None),
        P(("sub", "load"), None),
        P(),
        P(("sub", "load"), None, None),
        P(("sub", "load"), None, None),
        P(("sub", "load"), None, None),
        P(("sub", "load"), None),
        P("sub", "load"),
    )
    return jax.shard_map(
        on_device,
        mesh=mesh,
        in_specs=placed,
        out_specs=(P(("sub", "load"), None, None), P("sub", "load")),
        check_vma=False,
    )
```

```python
import functools
import math

import jax
import jax.numpy as jnp
from jax import lax
from jax.experimental import pallas as pl
from jax.experimental.pallas import tpu as pltpu
from jax.sharding import PartitionSpec as P

EDOF = 12
MODES = 12
SUB = 32
LOAD = 8
SPOTS = 1024
COLS = 128
UNKNOWNS = 1536
EDGE = 256
FIRST = 60
PART = 50
ENTRIES = SUB * LOAD * SPOTS
GRID_ROWS = 256
FIBRE_RATE = 0.3
ISO_RATE = 0.05
EPSILON = 1e-06

F32 = jnp.float32
BF16 = jnp.bfloat16


def call(kernel, outs, operands, name, flops=0, moved=16 * 2**20, limit=16, scratch=(), far=(), far_out=()):
    vmem, hbm = pl.BlockSpec(memory_space=pltpu.VMEM), pl.BlockSpec(memory_space=pltpu.HBM)
    return pl.pallas_call(
        kernel,
        in_specs=[hbm if place in far else vmem for place in range(len(operands))],
        out_specs=[hbm if place in far_out else vmem for place in range(len(outs))],
        out_shape=[jax.ShapeDtypeStruct(shape, dtype) for shape, dtype in outs],
        scratch_shapes=list(scratch),
        compiler_params=pltpu.CompilerParams(vmem_limit_bytes=int(limit * 2**20)),
        cost_estimate=pl.CostEstimate(flops=flops, bytes_accessed=moved, transcendentals=0),
        name=name,
    )(*operands)


def split2(value):
    high = value.astype(BF16)
    return high, (value - high.astype(F32)).astype(BF16)


def split3(value):
    high = value.astype(BF16)
    rest = value - high.astype(F32)
    middle = rest.astype(BF16)
    return high, middle, (rest - middle.astype(F32)).astype(BF16)


def dot(left, right):
    return jnp.dot(left, right, preferred_element_type=F32)


def lanes_of(shape):
    return lax.broadcasted_iota(jnp.int32, shape, 1)


def rows_of(shape):
    return lax.broadcasted_iota(jnp.int32, shape, 0)


def padded_basis(basis_ref, rows):
    basis = basis_ref[0].astype(F32)
    return jnp.concatenate([basis, jnp.zeros((rows - MODES, SPOTS), F32)], axis=0)


def coarse_rows(basis_ref, residual):
    basis = padded_basis(basis_ref, 16).astype(BF16)
    parts = dot(basis, jnp.concatenate(split3(residual), axis=1))
    terms = parts[:, :COLS] + parts[:, COLS : 2 * COLS] + parts[:, 2 * COLS :]
    squares = jnp.sum(residual * residual, axis=0, keepdims=True)
    return jnp.where(rows_of(terms.shape) == MODES, squares, terms)


def first_terms(
    rhs_hbm,
    basis_hbm,
    inverse_hbm,
    partner_hbm,
    out_ref,
    send_ref,
    lifted_ref,
    rhs_ref,
    basis_ref,
    inverse_ref,
    partner_ref,
    rhs_sem,
    basis_sem,
    inverse_sem,
    partner_sem,
):
    copies = [
        pltpu.make_async_copy(inverse_hbm, inverse_ref, inverse_sem),
        pltpu.make_async_copy(basis_hbm, basis_ref, basis_sem),
        pltpu.make_async_copy(rhs_hbm, rhs_ref, rhs_sem),
        pltpu.make_async_copy(partner_hbm, partner_ref, partner_sem),
    ]
    for copy in copies:
        copy.start()
    copies[0].wait()
    inverse = inverse_ref[...]
    inverse = jnp.concatenate([inverse, inverse[:, :128]], axis=1)
    pieces = []
    for group in range(SUB):
        start = group * LOAD * MODES
        tile, offset = start // 128, start % 128
        piece = inverse[:, 128 * tile : 128 * tile + 256]
        if offset:
            piece = pltpu.roll(piece, 256 - offset, axis=1)
        pieces.append(piece[:, :128])
    lanes = lanes_of((MODES, COLS))
    masks = [(lanes >= 16 * slot) & (lanes < 16 * slot + MODES) for slot in range(8)]
    for peer in range(LOAD):
        tiles = []
        for tile in range(4):
            chosen = jnp.zeros((MODES, COLS), F32)
            for slot in range(8):
                turn = (16 * slot - MODES * peer) % 128
                piece = pieces[8 * tile + slot]
                piece = pltpu.roll(piece, turn, axis=1) if turn else piece
                chosen = jnp.where(masks[slot], piece, chosen)
            tiles.append(chosen)
        out_ref[peer, 16:, :] = jnp.concatenate(tiles, axis=0)
    copies[3].wait()
    edge_rows(partner_ref[...].astype(F32), send_ref)
    copies[1].wait()
    basis = padded_basis(basis_ref, COLS).T
    basis = basis + pltpu.roll(basis, 16, axis=1) + pltpu.roll(basis, 32, axis=1)
    lifted_ref[...] = basis.astype(BF16)
    copies[2].wait()
    rows = coarse_rows(basis_ref, rhs_ref[0])
    for peer in range(LOAD):
        out_ref[peer, :16, :] = rows


def partial_rows(high, low, terms, out_ref):
    terms_high, terms_low = split2(terms)
    partial = dot(high, terms_high) + dot(high, terms_low) + dot(low, terms_high)
    out_ref[...] = partial.reshape(out_ref.shape)


def first_partial(received_ref, operator_hbm, out_ref, block_ref, operator_ref, operator_sem):
    copy = pltpu.make_async_copy(operator_hbm, operator_ref, operator_sem)
    copy.start()
    terms = received_ref[:, :16, :].reshape(LOAD * 16, COLS)
    lanes = lax.broadcasted_iota(jnp.int32, (LOAD, 4, COLS), 2)
    places = lax.broadcasted_iota(jnp.int32, (LOAD, 4, COLS), 1)
    mark = jnp.where((places == 0) & (lanes % 16 == MODES), 1.0, 0.0)
    tiles = []
    for tile in range(4):
        start = 16 + MODES * tile
        rows = jnp.concatenate([received_ref[:, start : start + MODES, :], mark], axis=1)
        tiles.append(rows.reshape(LOAD * 16, COLS))
    high, low = split2(jnp.concatenate(tiles, axis=1))
    block_ref[:, : SUB * 16] = high
    block_ref[:, SUB * 16 :] = low
    high, low = split2(jnp.concatenate([tile.T for tile in tiles], axis=0))
    partial_rows(high, low, terms, out_ref)
    copy.wait()


def later_partial(received_ref, block_ref, out_ref):
    terms = received_ref[...].reshape(SUB * 16, COLS)
    partial_rows(block_ref[:, : SUB * 16], block_ref[:, SUB * 16 :], terms, out_ref)


def class_partial(received_ref, block_ref, class_ref, out_ref, middle_ref):
    later_partial(received_ref, block_ref, out_ref)
    here = lax.axis_index("sub")
    above = received_ref[jnp.maximum(here - 1, 0)][14:15]
    below = received_ref[jnp.minimum(here + 1, SUB - 1)][13:14]
    above = jnp.where(here > 0, above, 0.0)
    below = jnp.where(here < SUB - 1, below, 0.0)
    classes = (class_ref[...] + 1).astype(F32)
    gap = jnp.zeros((1, COLS), F32)
    middle = jnp.concatenate([gap, above, classes, below, gap, gap, gap, gap, gap], axis=0)
    middle_ref[...] = middle
    sides = jnp.concatenate([middle, jnp.zeros((COLS - 16, COLS), F32)], axis=0).T
    for peer in range(LOAD):
        out_ref[peer, 13:14, :] = sides[0:1]
        out_ref[peer, 14:15, :] = sides[127:128]


def edge_rows(partners, send_ref):
    to_before = jnp.where(partners < SPOTS, 1.0, 0.0)
    to_after = jnp.where(partners >= 2 * SPOTS, 1.0, 0.0)
    sides = jnp.concatenate([to_before, to_after, jnp.zeros((6, SPOTS), F32)], axis=0)
    lanes = lanes_of(sides.shape)
    place = sides
    for power in range(10):
        earlier = pltpu.roll(place, 1 << power, axis=1)
        place = place + jnp.where(lanes >= 1 << power, earlier, 0.0)
    place = jnp.where(sides > 0.0, place - 1.0, -1.0)
    slots = rows_of((EDGE, SPOTS)).astype(F32)
    send_ref[:EDGE, :] = jnp.where(slots == place[0:1], 1.0, 0.0).astype(BF16)
    send_ref[EDGE:, :] = jnp.where(slots == place[1:2], 1.0, 0.0).astype(BF16)


def first_inner(images_ref, partner_ref, out_ref, pick_ref):
    partners = partner_ref[...].astype(F32)
    lanes = lanes_of((128, 128)).astype(F32)
    for block in range(SPOTS // 128):
        here = slice(128 * block, 128 * block + 128)
        wanted = jnp.broadcast_to(partners[:, here], (128, 128)).T
        smaller = jnp.zeros((128, 128), F32)
        for tile in range(SPOTS // 128):
            smaller = smaller + jnp.where(partners[:, 128 * tile : 128 * tile + 128] < wanted, 1.0, 0.0)
        rank = jnp.broadcast_to(jnp.sum(smaller, axis=1, keepdims=True), (128, 128))
        for tile in range((2 * EDGE + SPOTS) // 128):
            start = 128 * tile
            if start < EDGE:
                hit = rank == lanes + start
            elif start < EDGE + SPOTS:
                hit = wanted == lanes + (start - EDGE + SPOTS)
            else:
                hit = rank == lanes + (start - EDGE - SPOTS + 3 * EDGE)
            pick_ref[here, start : start + 128] = jnp.where(hit, 1.0, 0.0).astype(BF16)
    inner_pairs(images_ref, pick_ref, out_ref)


def step_parts(received_ref, damping_ref, lifted_ref):
    total = jnp.sum(received_ref[...], axis=0)
    step = damping_ref[...] / jnp.sqrt(total[MODES : MODES + 1] / ENTRIES + EPSILON)
    correction = jnp.where(rows_of(total.shape) < MODES, total, 0.0)
    stacked = jnp.concatenate(split3(correction) + (jnp.zeros((COLS - 48, COLS), BF16),), axis=0)
    return step, dot(lifted_ref[...], stacked)


def advance(first, received_ref, damping_ref, lifted_ref, operator_ref, send_ref, residual_ref, *rest):
    step, lifted = step_parts(received_ref, damping_ref, lifted_ref)
    if first:
        iterate_ref, images_ref, down_ref, up_ref = rest
        iterate = step * (residual_ref[0] - lifted)
    else:
        before_ref, iterate_ref, images_ref, down_ref, up_ref = rest
        iterate = before_ref[...] + step * (residual_ref[...] - lifted)
    iterate_ref[...] = iterate
    images = dot(operator_ref[0], iterate.astype(BF16)).astype(BF16)
    images_ref[...] = images
    edges = dot(send_ref[...], images).astype(BF16)
    down_ref[...] = edges[:EDGE]
    up_ref[...] = edges[EDGE:]


def inner_pairs(images_ref, pick_ref, out_ref):
    out_ref[...] = dot(pick_ref[:, EDGE : EDGE + SPOTS], images_ref[...])


def inner_classes(images_ref, pick_ref, received_ref, middle_ref, out_ref, classes_ref):
    here = lax.axis_index("load")
    right = received_ref[jnp.minimum(here + 1, LOAD - 1)][13:14]
    left = received_ref[jnp.maximum(here - 1, 0)][14:15]
    right = jnp.where(here < LOAD - 1, right, 0.0)
    left = jnp.where(here > 0, left, 0.0)
    right = jnp.broadcast_to(right, (128, 128)).T[:16]
    left = jnp.broadcast_to(left, (128, 128)).T[:16]
    lanes = lanes_of((16, 128))
    classes_ref[:, :128] = middle_ref[...]
    classes_ref[:, 128:] = jnp.where(lanes == 0, right, jnp.where(lanes == 127, left, 0.0))
    inner_pairs(images_ref, pick_ref, out_ref)


def residual_terms(
    rhs_ref, images_ref, inner_ref, pick_ref, before_ref, after_ref, basis_ref, class_ref, residual_ref, out_ref
):
    partners = inner_ref[...] + dot(pick_ref[:, :EDGE], before_ref[...])
    partners = partners + dot(pick_ref[:, EDGE + SPOTS :], after_ref[...])
    residual = rhs_ref[0] - (images_ref[...].astype(F32) + partners)
    residual_ref[...] = residual
    rows = coarse_rows(basis_ref, residual)
    classes = (class_ref[...] + 1).astype(F32)
    row = rows_of(rows.shape)
    rows = jnp.where(row == 13, classes[0:1], jnp.where(row == 14, classes[7:8], rows))
    for peer in range(SUB):
        out_ref[peer] = rows


def gradients(
    received_ref,
    damping_ref,
    lifted_ref,
    residual_ref,
    iterate_ref,
    recovery_ref,
    base_ref,
    adjoint_ref,
    voxel_ref,
    multipliers_hbm,
    out_ref,
    multipliers_ref,
    multipliers_sem,
):
    step, lifted = step_parts(received_ref, damping_ref, lifted_ref)
    multipliers = iterate_ref[...] + step * (residual_ref[...] - lifted)
    multipliers_ref[0] = multipliers
    copy = pltpu.make_async_copy(multipliers_ref, multipliers_hbm, multipliers_sem)
    copy.start()
    displaced = base_ref[0].astype(F32) - dot(recovery_ref[0], multipliers.astype(BF16))
    products = displaced * adjoint_ref[0].astype(F32)
    first = EDOF * rows_of((128, UNKNOWNS))
    lanes = lanes_of((128, UNKNOWNS))
    groups = jnp.where((lanes >= first) & (lanes < first + EDOF), 1.0, 0.0).astype(BF16)
    sums = dot(groups, jnp.concatenate(split2(products), axis=1))
    element = jnp.sum(sums, axis=1, keepdims=True) / math.sqrt(EDOF * COLS)
    voxel = voxel_ref[...]
    column = jnp.broadcast_to(voxel & 127, (128, 128)).astype(F32).T.astype(jnp.int32)
    placed = jnp.where(column == lanes_of((128, 128)), element, 0.0)
    rows = GRID_ROWS + 16
    at_row = jnp.where(rows_of((rows, 128)) - 2 == (voxel >> 7), 1.0, 0.0).astype(BF16)
    parts = dot(at_row, jnp.concatenate(split3(placed), axis=1))
    spread = parts[:, :COLS] + parts[:, COLS : 2 * COLS] + parts[:, 2 * COLS :]
    for peer in range(SUB):
        out_ref[peer] = spread[8 * peer : 8 * peer + 16]
    copy.wait()


def smooth(middle_ref, left_ref, right_ref, classes_ref, out_ref):
    beside = jnp.where(lanes_of((16, 128)) < 64, right_ref[...], left_ref[...])
    field = jnp.concatenate([middle_ref[...], beside], axis=1)
    classes = classes_ref[...]

    def moved(value, row, lane):
        if row:
            value = pltpu.roll(value, row % 16, axis=0)
        if lane:
            value = pltpu.roll(value, lane % 256, axis=1)
        return value

    for _ in range(2):
        twice = 2.0 * field
        up, down = moved(field, 1, 0), moved(field, -1, 0)
        along_rows = down + up - twice
        along_cols = moved(field, 0, -1) + moved(field, 0, 1) - twice
        diag_main = moved(down, 0, -1) + moved(up, 0, 1) - twice
        diag_anti = moved(down, 0, 1) + moved(up, 0, -1) - twice
        chosen = jnp.where(
            classes == 1.0,
            along_rows,
            jnp.where(classes == 2.0, along_cols, jnp.where(classes == 3.0, diag_main, diag_anti)),
        )
        field = field + FIBRE_RATE * chosen + ISO_RATE * (along_rows + along_cols)
        field = jnp.where(classes > 0.0, field, 0.0)
    out_ref[...] = field[2:10, :128]


def both_ways(value, axes, size, wrap):
    up = [(i, (i + 1) % size) for i in range(size if wrap else size - 1)]
    down = [(j, i) for i, j in up]
    return lax.ppermute(value, axes, up), lax.ppermute(value, axes, down)


def on_device(
    dual_ops,
    dual_rhs,
    partner,
    coarse_basis,
    coarse_inverse,
    damping,
    recovery,
    base_disp,
    adjoint,
    elem_voxel,
    fibre_class,
):
    damping = damping.reshape(1, COLS)
    tall = ((SPOTS, COLS), F32)
    to_sub = ((SUB, 16, COLS), F32)
    to_load = ((LOAD, 16, COLS), F32)
    edge = ((EDGE, COLS), BF16)
    whole = ("sub", "load")
    up = [(i, (i + 1) % (SUB * LOAD)) for i in range(SUB * LOAD)]
    down = [(j, i) for i, j in up]

    def over(value, axis):
        return lax.all_to_all(value, axis, 0, 0, tiled=True)

    sent, send, lifted = call(
        first_terms,
        [((LOAD, 64, COLS), F32), ((2 * EDGE, SPOTS), BF16), ((SPOTS, COLS), BF16)],
        (dual_rhs, coarse_basis, coarse_inverse, partner),
        "first_terms",
        scratch=[
            pltpu.VMEM(dual_rhs.shape, F32),
            pltpu.VMEM(coarse_basis.shape, BF16),
            pltpu.VMEM(coarse_inverse.shape, F32),
            pltpu.VMEM(partner.shape, jnp.int32),
        ]
        + [pltpu.SemaphoreType.DMA] * 4,
        far=(0, 1, 2, 3),
        limit=FIRST,
    )
    received = over(sent, "load")
    partial, block, operator = call(
        first_partial,
        [to_sub, ((COLS, 2 * SUB * 16), BF16), (dual_ops.shape, BF16)],
        (received, dual_ops),
        "first_partial",
        scratch=[pltpu.SemaphoreType.DMA],
        far=(1,),
        limit=PART,
    )
    residual = dual_rhs
    before = ()
    for iteration in range(2):
        received = over(partial, "load" if iteration else "sub")
        iterate, images, lower, upper = call(
            functools.partial(advance, iteration == 0),
            [tall, ((SPOTS, COLS), BF16), edge, edge],
            (received, damping, lifted, (operator, dual_ops)[iteration], send, residual) + before,
            "advance",
        )
        before = (iterate,)
        from_before = lax.ppermute(upper, whole, up)
        from_after = lax.ppermute(lower, whole, down)
        if iteration == 0:
            inner, pick = call(
                first_inner, [tall, ((SPOTS, SPOTS + 2 * EDGE), BF16)], (images, partner), "first_inner",
                flops=2 * SPOTS * SPOTS * 1024, moved=8 * 2**20,
            )
        else:
            inner, classes = call(
                inner_classes, [tall, ((16, 2 * COLS), F32)], (images, pick, received, middle), "inner_classes",
                flops=2 * SPOTS * SPOTS * 256, moved=4 * 2**20,
            )
        residual, sent = call(
            residual_terms,
            [tall, to_sub],
            (dual_rhs, images, inner, pick, from_before, from_after, coarse_basis, fibre_class),
            "residual_terms",
        )
        received = over(sent, "sub")
        if iteration == 0:
            partial, middle = call(
                class_partial, [to_load, ((16, COLS), F32)], (received, block, fibre_class), "class_partial"
            )
        else:
            (partial,) = call(later_partial, [to_load], (received, block), "later_partial")
    received = over(partial, "load")
    multipliers, sent = call(
        gradients,
        [((1, SPOTS, COLS), F32), to_sub],
        (received, damping, lifted, residual, iterate, recovery, base_disp, adjoint, elem_voxel),
        "gradients",
        scratch=[pltpu.VMEM((1, SPOTS, COLS), F32), pltpu.SemaphoreType.DMA],
        far_out=(0,),
    )
    middle = jnp.sum(over(sent, "sub"), axis=0)
    left, right = both_ways(middle, "load", LOAD, False)
    (field,) = call(
        smooth,
        [(fibre_class.shape, F32)],
        (middle, left, right, classes),
        "smooth",
    )
    return multipliers, field


def solution(mesh):
    placed = (
        P(("sub", "load"), None, None),
        P(("sub", "load"), None, None),
        P(("sub", "load"), None),
        P(("sub", "load"), None, None),
        P(("sub", "load"), None),
        P(),
        P(("sub", "load"), None, None),
        P(("sub", "load"), None, None),
        P(("sub", "load"), None, None),
        P(("sub", "load"), None),
        P("sub", "load"),
    )
    return jax.shard_map(
        on_device,
        mesh=mesh,
        in_specs=placed,
        out_specs=(P(("sub", "load"), None, None), P("sub", "load")),
        check_vma=False,
    )
```

```python
import functools
import math

import jax
import jax.numpy as jnp
from jax import lax
from jax.experimental import pallas as pl
from jax.experimental.pallas import tpu as pltpu
from jax.sharding import PartitionSpec as P

EDOF = 12
MODES = 12
SUB = 32
LOAD = 8
SPOTS = 1024
COLS = 128
UNKNOWNS = 1536
EDGE = 256
FIRST = 60
PART = 50
ENTRIES = SUB * LOAD * SPOTS
GRID_ROWS = 256
FIBRE_RATE = 0.3
ISO_RATE = 0.05
EPSILON = 1e-06

F32 = jnp.float32
BF16 = jnp.bfloat16


def call(kernel, outs, operands, name, flops=0, moved=16 * 2**20, limit=16, scratch=(), far=(), far_out=()):
    vmem, hbm = pl.BlockSpec(memory_space=pltpu.VMEM), pl.BlockSpec(memory_space=pltpu.HBM)
    return pl.pallas_call(
        kernel,
        in_specs=[hbm if place in far else vmem for place in range(len(operands))],
        out_specs=[hbm if place in far_out else vmem for place in range(len(outs))],
        out_shape=[jax.ShapeDtypeStruct(shape, dtype) for shape, dtype in outs],
        scratch_shapes=list(scratch),
        compiler_params=pltpu.CompilerParams(vmem_limit_bytes=int(limit * 2**20)),
        cost_estimate=pl.CostEstimate(flops=flops, bytes_accessed=moved, transcendentals=0),
        name=name,
    )(*operands)


def split2(value):
    high = value.astype(BF16)
    return high, (value - high.astype(F32)).astype(BF16)


def split3(value):
    high = value.astype(BF16)
    rest = value - high.astype(F32)
    middle = rest.astype(BF16)
    return high, middle, (rest - middle.astype(F32)).astype(BF16)


def dot(left, right):
    return jnp.dot(left, right, preferred_element_type=F32)


def lanes_of(shape):
    return lax.broadcasted_iota(jnp.int32, shape, 1)


def rows_of(shape):
    return lax.broadcasted_iota(jnp.int32, shape, 0)


def padded_basis(basis_ref, rows):
    basis = basis_ref[0].astype(F32)
    return jnp.concatenate([basis, jnp.zeros((rows - MODES, SPOTS), F32)], axis=0)


def coarse_rows(basis_ref, residual):
    basis = padded_basis(basis_ref, 16).astype(BF16)
    parts = dot(basis, jnp.concatenate(split3(residual), axis=1))
    terms = parts[:, :COLS] + parts[:, COLS : 2 * COLS] + parts[:, 2 * COLS :]
    squares = jnp.sum(residual * residual, axis=0, keepdims=True)
    return jnp.where(rows_of(terms.shape) == MODES, squares, terms)


def first_terms(
    rhs_hbm,
    basis_hbm,
    inverse_hbm,
    partner_hbm,
    out_hbm,
    send_hbm,
    lifted_hbm,
    rhs_ref,
    basis_ref,
    inverse_ref,
    partner_ref,
    out_ref,
    send_ref,
    lifted_ref,
    rhs_sem,
    basis_sem,
    inverse_sem,
    partner_sem,
    rows_sem,
    tiles_sem,
    send_sem,
    lifted_sem,
):
    results = [
        pltpu.make_async_copy(out_ref.at[:, pl.ds(16, 48), :], out_hbm.at[:, pl.ds(16, 48), :], tiles_sem),
        pltpu.make_async_copy(send_ref, send_hbm, send_sem),
        pltpu.make_async_copy(lifted_ref, lifted_hbm, lifted_sem),
        pltpu.make_async_copy(out_ref.at[:, pl.ds(0, 16), :], out_hbm.at[:, pl.ds(0, 16), :], rows_sem),
    ]
    copies = [
        pltpu.make_async_copy(inverse_hbm, inverse_ref, inverse_sem),
        pltpu.make_async_copy(basis_hbm, basis_ref, basis_sem),
        pltpu.make_async_copy(rhs_hbm, rhs_ref, rhs_sem),
        pltpu.make_async_copy(partner_hbm, partner_ref, partner_sem),
    ]
    for copy in copies:
        copy.start()
    copies[0].wait()
    inverse = inverse_ref[...]
    inverse = jnp.concatenate([inverse, inverse[:, :128]], axis=1)
    pieces = []
    for group in range(SUB):
        start = group * LOAD * MODES
        tile, offset = start // 128, start % 128
        piece = inverse[:, 128 * tile : 128 * tile + 256]
        if offset:
            piece = pltpu.roll(piece, 256 - offset, axis=1)
        pieces.append(piece[:, :128])
    lanes = lanes_of((MODES, COLS))
    masks = [(lanes >= 16 * slot) & (lanes < 16 * slot + MODES) for slot in range(8)]
    for peer in range(LOAD):
        tiles = []
        for tile in range(4):
            chosen = jnp.zeros((MODES, COLS), F32)
            for slot in range(8):
                turn = (16 * slot - MODES * peer) % 128
                piece = pieces[8 * tile + slot]
                piece = pltpu.roll(piece, turn, axis=1) if turn else piece
                chosen = jnp.where(masks[slot], piece, chosen)
            tiles.append(chosen)
        out_ref[peer, 16:, :] = jnp.concatenate(tiles, axis=0)
    results[0].start()
    copies[3].wait()
    edge_rows(partner_ref[...].astype(F32), send_ref)
    results[1].start()
    copies[1].wait()
    basis = padded_basis(basis_ref, COLS).T
    basis = basis + pltpu.roll(basis, 16, axis=1) + pltpu.roll(basis, 32, axis=1)
    lifted_ref[...] = basis.astype(BF16)
    results[2].start()
    copies[2].wait()
    rows = coarse_rows(basis_ref, rhs_ref[0])
    for peer in range(LOAD):
        out_ref[peer, :16, :] = rows
    results[3].start()
    for copy in results:
        copy.wait()


def partial_rows(high, low, terms, out_ref):
    terms_high, terms_low = split2(terms)
    partial = dot(high, terms_high) + dot(high, terms_low) + dot(low, terms_high)
    out_ref[...] = partial.reshape(out_ref.shape)


def first_partial(received_ref, operator_hbm, out_ref, block_ref, operator_ref, operator_sem):
    copy = pltpu.make_async_copy(operator_hbm, operator_ref, operator_sem)
    copy.start()
    terms = received_ref[:, :16, :].reshape(LOAD * 16, COLS)
    lanes = lax.broadcasted_iota(jnp.int32, (LOAD, 4, COLS), 2)
    places = lax.broadcasted_iota(jnp.int32, (LOAD, 4, COLS), 1)
    mark = jnp.where((places == 0) & (lanes % 16 == MODES), 1.0, 0.0)
    tiles = []
    for tile in range(4):
        start = 16 + MODES * tile
        rows = jnp.concatenate([received_ref[:, start : start + MODES, :], mark], axis=1)
        tiles.append(rows.reshape(LOAD * 16, COLS))
    high, low = split2(jnp.concatenate(tiles, axis=1))
    block_ref[:, : SUB * 16] = high
    block_ref[:, SUB * 16 :] = low
    high, low = split2(jnp.concatenate([tile.T for tile in tiles], axis=0))
    partial_rows(high, low, terms, out_ref)
    copy.wait()


def later_partial(received_ref, block_ref, out_ref):
    terms = received_ref[...].reshape(SUB * 16, COLS)
    partial_rows(block_ref[:, : SUB * 16], block_ref[:, SUB * 16 :], terms, out_ref)


def class_partial(received_ref, block_ref, class_ref, out_ref, middle_ref):
    later_partial(received_ref, block_ref, out_ref)
    here = lax.axis_index("sub")
    above = received_ref[jnp.maximum(here - 1, 0)][14:15]
    below = received_ref[jnp.minimum(here + 1, SUB - 1)][13:14]
    above = jnp.where(here > 0, above, 0.0)
    below = jnp.where(here < SUB - 1, below, 0.0)
    classes = (class_ref[...] + 1).astype(F32)
    gap = jnp.zeros((1, COLS), F32)
    middle = jnp.concatenate([gap, above, classes, below, gap, gap, gap, gap, gap], axis=0)
    middle_ref[...] = middle
    sides = jnp.concatenate([middle, jnp.zeros((COLS - 16, COLS), F32)], axis=0).T
    for peer in range(LOAD):
        out_ref[peer, 13:14, :] = sides[0:1]
        out_ref[peer, 14:15, :] = sides[127:128]


def edge_rows(partners, send_ref):
    to_before = jnp.where(partners < SPOTS, 1.0, 0.0)
    to_after = jnp.where(partners >= 2 * SPOTS, 1.0, 0.0)
    sides = jnp.concatenate([to_before, to_after, jnp.zeros((6, SPOTS), F32)], axis=0)
    lanes = lanes_of(sides.shape)
    place = sides
    for power in range(10):
        earlier = pltpu.roll(place, 1 << power, axis=1)
        place = place + jnp.where(lanes >= 1 << power, earlier, 0.0)
    place = jnp.where(sides > 0.0, place - 1.0, -1.0)
    slots = rows_of((EDGE, SPOTS)).astype(F32)
    send_ref[:EDGE, :] = jnp.where(slots == place[0:1], 1.0, 0.0).astype(BF16)
    send_ref[EDGE:, :] = jnp.where(slots == place[1:2], 1.0, 0.0).astype(BF16)


def first_inner(images_ref, partner_ref, out_ref, pick_ref):
    partners = partner_ref[...].astype(F32)
    lanes = lanes_of((128, 128)).astype(F32)
    for block in range(SPOTS // 128):
        here = slice(128 * block, 128 * block + 128)
        wanted = jnp.broadcast_to(partners[:, here], (128, 128)).T
        smaller = jnp.zeros((128, 128), F32)
        for tile in range(SPOTS // 128):
            smaller = smaller + jnp.where(partners[:, 128 * tile : 128 * tile + 128] < wanted, 1.0, 0.0)
        rank = jnp.broadcast_to(jnp.sum(smaller, axis=1, keepdims=True), (128, 128))
        for tile in range((2 * EDGE + SPOTS) // 128):
            start = 128 * tile
            if start < EDGE:
                hit = rank == lanes + start
            elif start < EDGE + SPOTS:
                hit = wanted == lanes + (start - EDGE + SPOTS)
            else:
                hit = rank == lanes + (start - EDGE - SPOTS + 3 * EDGE)
            pick_ref[here, start : start + 128] = jnp.where(hit, 1.0, 0.0).astype(BF16)
    inner_pairs(images_ref, pick_ref, out_ref)


def step_parts(received_ref, damping_ref, lifted_ref):
    total = jnp.sum(received_ref[...], axis=0)
    step = damping_ref[...] / jnp.sqrt(total[MODES : MODES + 1] / ENTRIES + EPSILON)
    correction = jnp.where(rows_of(total.shape) < MODES, total, 0.0)
    stacked = jnp.concatenate(split3(correction) + (jnp.zeros((COLS - 48, COLS), BF16),), axis=0)
    return step, dot(lifted_ref[...], stacked)


def advance(first, received_ref, damping_ref, lifted_ref, operator_ref, send_ref, residual_ref, *rest):
    step, lifted = step_parts(received_ref, damping_ref, lifted_ref)
    if first:
        iterate_ref, images_ref, down_ref, up_ref = rest
        iterate = step * (residual_ref[0] - lifted)
    else:
        before_ref, iterate_ref, images_ref, down_ref, up_ref = rest
        iterate = before_ref[...] + step * (residual_ref[...] - lifted)
    iterate_ref[...] = iterate
    images = dot(operator_ref[0], iterate.astype(BF16)).astype(BF16)
    images_ref[...] = images
    edges = dot(send_ref[...], images).astype(BF16)
    down_ref[...] = edges[:EDGE]
    up_ref[...] = edges[EDGE:]


def inner_pairs(images_ref, pick_ref, out_ref):
    out_ref[...] = dot(pick_ref[:, EDGE : EDGE + SPOTS], images_ref[...])


def inner_classes(images_ref, pick_ref, received_ref, middle_ref, out_ref, classes_ref):
    here = lax.axis_index("load")
    right = received_ref[jnp.minimum(here + 1, LOAD - 1)][13:14]
    left = received_ref[jnp.maximum(here - 1, 0)][14:15]
    right = jnp.where(here < LOAD - 1, right, 0.0)
    left = jnp.where(here > 0, left, 0.0)
    right = jnp.broadcast_to(right, (128, 128)).T[:16]
    left = jnp.broadcast_to(left, (128, 128)).T[:16]
    lanes = lanes_of((16, 128))
    classes_ref[:, :128] = middle_ref[...]
    classes_ref[:, 128:] = jnp.where(lanes == 0, right, jnp.where(lanes == 127, left, 0.0))
    inner_pairs(images_ref, pick_ref, out_ref)


def residual_terms(
    rhs_ref, images_ref, inner_ref, pick_ref, before_ref, after_ref, basis_ref, class_ref, residual_ref, out_ref
):
    partners = inner_ref[...] + dot(pick_ref[:, :EDGE], before_ref[...])
    partners = partners + dot(pick_ref[:, EDGE + SPOTS :], after_ref[...])
    residual = rhs_ref[0] - (images_ref[...].astype(F32) + partners)
    residual_ref[...] = residual
    rows = coarse_rows(basis_ref, residual)
    classes = (class_ref[...] + 1).astype(F32)
    row = rows_of(rows.shape)
    rows = jnp.where(row == 13, classes[0:1], jnp.where(row == 14, classes[7:8], rows))
    for peer in range(SUB):
        out_ref[peer] = rows


def gradients(
    received_ref,
    damping_ref,
    lifted_ref,
    residual_ref,
    iterate_ref,
    recovery_ref,
    base_ref,
    adjoint_ref,
    voxel_ref,
    multipliers_hbm,
    out_ref,
    multipliers_ref,
    multipliers_sem,
):
    step, lifted = step_parts(received_ref, damping_ref, lifted_ref)
    multipliers = iterate_ref[...] + step * (residual_ref[...] - lifted)
    multipliers_ref[0] = multipliers
    copy = pltpu.make_async_copy(multipliers_ref, multipliers_hbm, multipliers_sem)
    copy.start()
    displaced = base_ref[0].astype(F32) - dot(recovery_ref[0], multipliers.astype(BF16))
    products = displaced * adjoint_ref[0].astype(F32)
    first = EDOF * rows_of((128, UNKNOWNS))
    lanes = lanes_of((128, UNKNOWNS))
    groups = jnp.where((lanes >= first) & (lanes < first + EDOF), 1.0, 0.0).astype(BF16)
    sums = dot(groups, jnp.concatenate(split2(products), axis=1))
    element = jnp.sum(sums, axis=1, keepdims=True) / math.sqrt(EDOF * COLS)
    voxel = voxel_ref[...]
    column = jnp.broadcast_to(voxel & 127, (128, 128)).astype(F32).T.astype(jnp.int32)
    placed = jnp.where(column == lanes_of((128, 128)), element, 0.0)
    rows = GRID_ROWS + 16
    at_row = jnp.where(rows_of((rows, 128)) - 2 == (voxel >> 7), 1.0, 0.0).astype(BF16)
    parts = dot(at_row, jnp.concatenate(split3(placed), axis=1))
    spread = parts[:, :COLS] + parts[:, COLS : 2 * COLS] + parts[:, 2 * COLS :]
    for peer in range(SUB):
        out_ref[peer] = spread[8 * peer : 8 * peer + 16]
    copy.wait()


def smooth(middle_ref, left_ref, right_ref, classes_ref, out_ref):
    beside = jnp.where(lanes_of((16, 128)) < 64, right_ref[...], left_ref[...])
    field = jnp.concatenate([middle_ref[...], beside], axis=1)
    classes = classes_ref[...]

    def moved(value, row, lane):
        if row:
            value = pltpu.roll(value, row % 16, axis=0)
        if lane:
            value = pltpu.roll(value, lane % 256, axis=1)
        return value

    for _ in range(2):
        twice = 2.0 * field
        up, down = moved(field, 1, 0), moved(field, -1, 0)
        along_rows = down + up - twice
        along_cols = moved(field, 0, -1) + moved(field, 0, 1) - twice
        diag_main = moved(down, 0, -1) + moved(up, 0, 1) - twice
        diag_anti = moved(down, 0, 1) + moved(up, 0, -1) - twice
        chosen = jnp.where(
            classes == 1.0,
            along_rows,
            jnp.where(classes == 2.0, along_cols, jnp.where(classes == 3.0, diag_main, diag_anti)),
        )
        field = field + FIBRE_RATE * chosen + ISO_RATE * (along_rows + along_cols)
        field = jnp.where(classes > 0.0, field, 0.0)
    out_ref[...] = field[2:10, :128]


def both_ways(value, axes, size, wrap):
    up = [(i, (i + 1) % size) for i in range(size if wrap else size - 1)]
    down = [(j, i) for i, j in up]
    return lax.ppermute(value, axes, up), lax.ppermute(value, axes, down)


def on_device(
    dual_ops,
    dual_rhs,
    partner,
    coarse_basis,
    coarse_inverse,
    damping,
    recovery,
    base_disp,
    adjoint,
    elem_voxel,
    fibre_class,
):
    damping = damping.reshape(1, COLS)
    tall = ((SPOTS, COLS), F32)
    to_sub = ((SUB, 16, COLS), F32)
    to_load = ((LOAD, 16, COLS), F32)
    edge = ((EDGE, COLS), BF16)
    whole = ("sub", "load")
    up = [(i, (i + 1) % (SUB * LOAD)) for i in range(SUB * LOAD)]
    down = [(j, i) for i, j in up]

    def over(value, axis):
        return lax.all_to_all(value, axis, 0, 0, tiled=True)

    sent, send, lifted = call(
        first_terms,
        [((LOAD, 64, COLS), F32), ((2 * EDGE, SPOTS), BF16), ((SPOTS, COLS), BF16)],
        (dual_rhs, coarse_basis, coarse_inverse, partner),
        "first_terms",
        scratch=[
            pltpu.VMEM(dual_rhs.shape, F32),
            pltpu.VMEM(coarse_basis.shape, BF16),
            pltpu.VMEM(coarse_inverse.shape, F32),
            pltpu.VMEM(partner.shape, jnp.int32),
            pltpu.VMEM((LOAD, 64, COLS), F32),
            pltpu.VMEM((2 * EDGE, SPOTS), BF16),
            pltpu.VMEM((SPOTS, COLS), BF16),
        ]
        + [pltpu.SemaphoreType.DMA] * 8,
        far=(0, 1, 2, 3),
        far_out=(0, 1, 2),
        limit=FIRST,
    )
    received = over(sent, "load")
    partial, block, operator = call(
        first_partial,
        [to_sub, ((COLS, 2 * SUB * 16), BF16), (dual_ops.shape, BF16)],
        (received, dual_ops),
        "first_partial",
        scratch=[pltpu.SemaphoreType.DMA],
        far=(1,),
        limit=PART,
    )
    residual = dual_rhs
    before = ()
    for iteration in range(2):
        received = over(partial, "load" if iteration else "sub")
        iterate, images, lower, upper = call(
            functools.partial(advance, iteration == 0),
            [tall, ((SPOTS, COLS), BF16), edge, edge],
            (received, damping, lifted, (operator, dual_ops)[iteration], send, residual) + before,
            "advance",
        )
        before = (iterate,)
        from_before = lax.ppermute(upper, whole, up)
        from_after = lax.ppermute(lower, whole, down)
        if iteration == 0:
            inner, pick = call(
                first_inner, [tall, ((SPOTS, SPOTS + 2 * EDGE), BF16)], (images, partner), "first_inner",
                flops=2 * SPOTS * SPOTS * 1024, moved=8 * 2**20,
            )
        else:
            inner, classes = call(
                inner_classes, [tall, ((16, 2 * COLS), F32)], (images, pick, received, middle), "inner_classes",
                flops=2 * SPOTS * SPOTS * 256, moved=4 * 2**20,
            )
        residual, sent = call(
            residual_terms,
            [tall, to_sub],
            (dual_rhs, images, inner, pick, from_before, from_after, coarse_basis, fibre_class),
            "residual_terms",
        )
        received = over(sent, "sub")
        if iteration == 0:
            partial, middle = call(
                class_partial, [to_load, ((16, COLS), F32)], (received, block, fibre_class), "class_partial"
            )
        else:
            (partial,) = call(later_partial, [to_load], (received, block), "later_partial")
    received = over(partial, "load")
    multipliers, sent = call(
        gradients,
        [((1, SPOTS, COLS), F32), to_sub],
        (received, damping, lifted, residual, iterate, recovery, base_disp, adjoint, elem_voxel),
        "gradients",
        scratch=[pltpu.VMEM((1, SPOTS, COLS), F32), pltpu.SemaphoreType.DMA],
        far_out=(0,),
    )
    middle = jnp.sum(over(sent, "sub"), axis=0)
    left, right = both_ways(middle, "load", LOAD, False)
    (field,) = call(
        smooth,
        [(fibre_class.shape, F32)],
        (middle, left, right, classes),
        "smooth",
    )
    return multipliers, field


def solution(mesh):
    placed = (
        P(("sub", "load"), None, None),
        P(("sub", "load"), None, None),
        P(("sub", "load"), None),
        P(("sub", "load"), None, None),
        P(("sub", "load"), None),
        P(),
        P(("sub", "load"), None, None),
        P(("sub", "load"), None, None),
        P(("sub", "load"), None, None),
        P(("sub", "load"), None),
        P("sub", "load"),
    )
    return jax.shard_map(
        on_device,
        mesh=mesh,
        in_specs=placed,
        out_specs=(P(("sub", "load"), None, None), P("sub", "load")),
        check_vma=False,
    )
```

```python
import functools
import math

import jax
import jax.numpy as jnp
from jax import lax
from jax.experimental import pallas as pl
from jax.experimental.pallas import tpu as pltpu
from jax.sharding import PartitionSpec as P

EDOF = 12
MODES = 12
SUB = 32
LOAD = 8
SPOTS = 1024
COLS = 128
UNKNOWNS = 1536
EDGE = 256
FIRST = 60
PART = 50
ENTRIES = SUB * LOAD * SPOTS
GRID_ROWS = 256
FIBRE_RATE = 0.3
ISO_RATE = 0.05
EPSILON = 1e-06

F32 = jnp.float32
BF16 = jnp.bfloat16


def call(kernel, outs, operands, name, flops=0, moved=16 * 2**20, limit=16, scratch=(), far=(), far_out=()):
    vmem, hbm = pl.BlockSpec(memory_space=pltpu.VMEM), pl.BlockSpec(memory_space=pltpu.HBM)
    return pl.pallas_call(
        kernel,
        in_specs=[hbm if place in far else vmem for place in range(len(operands))],
        out_specs=[hbm if place in far_out else vmem for place in range(len(outs))],
        out_shape=[jax.ShapeDtypeStruct(shape, dtype) for shape, dtype in outs],
        scratch_shapes=list(scratch),
        compiler_params=pltpu.CompilerParams(vmem_limit_bytes=int(limit * 2**20)),
        cost_estimate=pl.CostEstimate(flops=flops, bytes_accessed=moved, transcendentals=0),
        name=name,
    )(*operands)


def split2(value):
    high = value.astype(BF16)
    return high, (value - high.astype(F32)).astype(BF16)


def split3(value):
    high = value.astype(BF16)
    rest = value - high.astype(F32)
    middle = rest.astype(BF16)
    return high, middle, (rest - middle.astype(F32)).astype(BF16)


def dot(left, right):
    return jnp.dot(left, right, preferred_element_type=F32)


def lanes_of(shape):
    return lax.broadcasted_iota(jnp.int32, shape, 1)


def rows_of(shape):
    return lax.broadcasted_iota(jnp.int32, shape, 0)


def padded_basis(basis_ref, rows):
    basis = basis_ref[0].astype(F32)
    return jnp.concatenate([basis, jnp.zeros((rows - MODES, SPOTS), F32)], axis=0)


def coarse_rows(basis_ref, residual):
    basis = padded_basis(basis_ref, 16).astype(BF16)
    parts = dot(basis, jnp.concatenate(split3(residual), axis=1))
    terms = parts[:, :COLS] + parts[:, COLS : 2 * COLS] + parts[:, 2 * COLS :]
    squares = jnp.sum(residual * residual, axis=0, keepdims=True)
    return jnp.where(rows_of(terms.shape) == MODES, squares, terms)


def first_terms(
    rhs_hbm,
    basis_hbm,
    inverse_hbm,
    partner_hbm,
    out_hbm,
    send_hbm,
    lifted_hbm,
    rhs_ref,
    basis_ref,
    inverse_ref,
    partner_ref,
    out_ref,
    send_ref,
    lifted_ref,
    rhs_sem,
    basis_sem,
    inverse_sem,
    partner_sem,
    rows_sem,
    tiles_sem,
    send_sem,
    lifted_sem,
):
    results = [
        pltpu.make_async_copy(out_ref.at[:, pl.ds(16, 48), :], out_hbm.at[:, pl.ds(16, 48), :], tiles_sem),
        pltpu.make_async_copy(send_ref, send_hbm, send_sem),
        pltpu.make_async_copy(lifted_ref, lifted_hbm, lifted_sem),
        pltpu.make_async_copy(out_ref.at[:, pl.ds(0, 16), :], out_hbm.at[:, pl.ds(0, 16), :], rows_sem),
    ]
    copies = [
        pltpu.make_async_copy(inverse_hbm, inverse_ref, inverse_sem),
        pltpu.make_async_copy(basis_hbm, basis_ref, basis_sem),
        pltpu.make_async_copy(rhs_hbm, rhs_ref, rhs_sem),
        pltpu.make_async_copy(partner_hbm, partner_ref, partner_sem),
    ]
    for copy in copies:
        copy.start()
    copies[0].wait()
    inverse = inverse_ref[...]
    inverse = jnp.concatenate([inverse, inverse[:, :128]], axis=1)
    pieces = []
    for group in range(SUB):
        start = group * LOAD * MODES
        tile, offset = start // 128, start % 128
        piece = inverse[:, 128 * tile : 128 * tile + 256]
        if offset:
            piece = pltpu.roll(piece, 256 - offset, axis=1)
        pieces.append(piece[:, :128])
    lanes = lanes_of((MODES, COLS))
    masks = [(lanes >= 16 * slot) & (lanes < 16 * slot + MODES) for slot in range(8)]
    for peer in range(LOAD):
        tiles = []
        for tile in range(4):
            chosen = jnp.zeros((MODES, COLS), F32)
            for slot in range(8):
                turn = (16 * slot - MODES * peer) % 128
                piece = pieces[8 * tile + slot]
                piece = pltpu.roll(piece, turn, axis=1) if turn else piece
                chosen = jnp.where(masks[slot], piece, chosen)
            tiles.append(chosen)
        out_ref[peer, 16:, :] = jnp.concatenate(tiles, axis=0)
    results[0].start()
    copies[3].wait()
    edge_rows(partner_ref[...].astype(F32), send_ref)
    results[1].start()
    copies[1].wait()
    basis = padded_basis(basis_ref, COLS).T
    basis = basis + pltpu.roll(basis, 16, axis=1) + pltpu.roll(basis, 32, axis=1)
    lifted_ref[...] = basis.astype(BF16)
    results[2].start()
    copies[2].wait()
    rows = coarse_rows(basis_ref, rhs_ref[0])
    for peer in range(LOAD):
        out_ref[peer, :16, :] = rows
    results[3].start()
    for copy in results:
        copy.wait()


def partial_rows(high, low, terms, out_ref):
    terms_high, terms_low = split2(terms)
    partial = dot(high, terms_high) + dot(high, terms_low) + dot(low, terms_high)
    out_ref[...] = partial.reshape(out_ref.shape)


def first_partial(received_ref, operator_hbm, out_ref, block_ref, operator_ref, *operator_sems):
    copies = []
    for part, semaphore in enumerate(operator_sems):
        rows = pl.ds(256 * part, 256)
        copies.append(pltpu.make_async_copy(operator_hbm.at[:, rows, :], operator_ref.at[:, rows, :], semaphore))
    for copy in copies:
        copy.start()
    terms = received_ref[:, :16, :].reshape(LOAD * 16, COLS)
    lanes = lax.broadcasted_iota(jnp.int32, (LOAD, 4, COLS), 2)
    places = lax.broadcasted_iota(jnp.int32, (LOAD, 4, COLS), 1)
    mark = jnp.where((places == 0) & (lanes % 16 == MODES), 1.0, 0.0)
    tiles = []
    for tile in range(4):
        start = 16 + MODES * tile
        rows = jnp.concatenate([received_ref[:, start : start + MODES, :], mark], axis=1)
        tiles.append(rows.reshape(LOAD * 16, COLS))
    high, low = split2(jnp.concatenate(tiles, axis=1))
    block_ref[:, : SUB * 16] = high
    block_ref[:, SUB * 16 :] = low
    high, low = split2(jnp.concatenate([tile.T for tile in tiles], axis=0))
    partial_rows(high, low, terms, out_ref)
    for copy in copies:
        copy.wait()


def later_partial(received_ref, block_ref, out_ref):
    terms = received_ref[...].reshape(SUB * 16, COLS)
    partial_rows(block_ref[:, : SUB * 16], block_ref[:, SUB * 16 :], terms, out_ref)


def class_partial(received_ref, block_ref, class_ref, out_ref, middle_ref):
    later_partial(received_ref, block_ref, out_ref)
    here = lax.axis_index("sub")
    above = received_ref[jnp.maximum(here - 1, 0)][14:15]
    below = received_ref[jnp.minimum(here + 1, SUB - 1)][13:14]
    above = jnp.where(here > 0, above, 0.0)
    below = jnp.where(here < SUB - 1, below, 0.0)
    classes = (class_ref[...] + 1).astype(F32)
    gap = jnp.zeros((1, COLS), F32)
    middle = jnp.concatenate([gap, above, classes, below, gap, gap, gap, gap, gap], axis=0)
    middle_ref[...] = middle
    sides = jnp.concatenate([middle, jnp.zeros((COLS - 16, COLS), F32)], axis=0).T
    for peer in range(LOAD):
        out_ref[peer, 13:14, :] = sides[0:1]
        out_ref[peer, 14:15, :] = sides[127:128]


def edge_rows(partners, send_ref):
    to_before = jnp.where(partners < SPOTS, 1.0, 0.0)
    to_after = jnp.where(partners >= 2 * SPOTS, 1.0, 0.0)
    sides = jnp.concatenate([to_before, to_after, jnp.zeros((6, SPOTS), F32)], axis=0)
    lanes = lanes_of(sides.shape)
    place = sides
    for power in range(10):
        earlier = pltpu.roll(place, 1 << power, axis=1)
        place = place + jnp.where(lanes >= 1 << power, earlier, 0.0)
    place = jnp.where(sides > 0.0, place - 1.0, -1.0)
    slots = rows_of((EDGE, SPOTS)).astype(F32)
    send_ref[:EDGE, :] = jnp.where(slots == place[0:1], 1.0, 0.0).astype(BF16)
    send_ref[EDGE:, :] = jnp.where(slots == place[1:2], 1.0, 0.0).astype(BF16)


def first_inner(images_ref, partner_ref, out_ref, pick_ref):
    partners = partner_ref[...].astype(F32)
    lanes = lanes_of((128, 128)).astype(F32)
    for block in range(SPOTS // 128):
        here = slice(128 * block, 128 * block + 128)
        wanted = jnp.broadcast_to(partners[:, here], (128, 128)).T
        smaller = jnp.zeros((128, 128), F32)
        for tile in range(SPOTS // 128):
            smaller = smaller + jnp.where(partners[:, 128 * tile : 128 * tile + 128] < wanted, 1.0, 0.0)
        rank = jnp.broadcast_to(jnp.sum(smaller, axis=1, keepdims=True), (128, 128))
        for tile in range((2 * EDGE + SPOTS) // 128):
            start = 128 * tile
            if start < EDGE:
                hit = rank == lanes + start
            elif start < EDGE + SPOTS:
                hit = wanted == lanes + (start - EDGE + SPOTS)
            else:
                hit = rank == lanes + (start - EDGE - SPOTS + 3 * EDGE)
            pick_ref[here, start : start + 128] = jnp.where(hit, 1.0, 0.0).astype(BF16)
    inner_pairs(images_ref, pick_ref, out_ref)


def step_parts(received_ref, damping_ref, lifted_ref):
    total = jnp.sum(received_ref[...], axis=0)
    step = damping_ref[...] / jnp.sqrt(total[MODES : MODES + 1] / ENTRIES + EPSILON)
    correction = jnp.where(rows_of(total.shape) < MODES, total, 0.0)
    stacked = jnp.concatenate(split3(correction) + (jnp.zeros((COLS - 48, COLS), BF16),), axis=0)
    return step, dot(lifted_ref[...], stacked)


def advance(first, received_ref, damping_ref, lifted_ref, operator_ref, send_ref, residual_ref, *rest):
    step, lifted = step_parts(received_ref, damping_ref, lifted_ref)
    if first:
        iterate_ref, images_ref, down_ref, up_ref = rest
        iterate = step * (residual_ref[0] - lifted)
    else:
        before_ref, iterate_ref, images_ref, down_ref, up_ref = rest
        iterate = before_ref[...] + step * (residual_ref[...] - lifted)
    iterate_ref[...] = iterate
    images = dot(operator_ref[0], iterate.astype(BF16)).astype(BF16)
    images_ref[...] = images
    edges = dot(send_ref[...], images).astype(BF16)
    down_ref[...] = edges[:EDGE]
    up_ref[...] = edges[EDGE:]


def inner_pairs(images_ref, pick_ref, out_ref):
    out_ref[...] = dot(pick_ref[:, EDGE : EDGE + SPOTS], images_ref[...])


def inner_classes(images_ref, pick_ref, received_ref, middle_ref, out_ref, classes_ref):
    here = lax.axis_index("load")
    right = received_ref[jnp.minimum(here + 1, LOAD - 1)][13:14]
    left = received_ref[jnp.maximum(here - 1, 0)][14:15]
    right = jnp.where(here < LOAD - 1, right, 0.0)
    left = jnp.where(here > 0, left, 0.0)
    right = jnp.broadcast_to(right, (128, 128)).T[:16]
    left = jnp.broadcast_to(left, (128, 128)).T[:16]
    lanes = lanes_of((16, 128))
    classes_ref[:, :128] = middle_ref[...]
    classes_ref[:, 128:] = jnp.where(lanes == 0, right, jnp.where(lanes == 127, left, 0.0))
    inner_pairs(images_ref, pick_ref, out_ref)


def residual_terms(
    rhs_ref, images_ref, inner_ref, pick_ref, before_ref, after_ref, basis_ref, class_ref, residual_ref, out_ref
):
    partners = inner_ref[...] + dot(pick_ref[:, :EDGE], before_ref[...])
    partners = partners + dot(pick_ref[:, EDGE + SPOTS :], after_ref[...])
    residual = rhs_ref[0] - (images_ref[...].astype(F32) + partners)
    residual_ref[...] = residual
    rows = coarse_rows(basis_ref, residual)
    classes = (class_ref[...] + 1).astype(F32)
    row = rows_of(rows.shape)
    rows = jnp.where(row == 13, classes[0:1], jnp.where(row == 14, classes[7:8], rows))
    for peer in range(SUB):
        out_ref[peer] = rows


def gradients(
    received_ref,
    damping_ref,
    lifted_ref,
    residual_ref,
    iterate_ref,
    recovery_ref,
    base_ref,
    adjoint_ref,
    voxel_ref,
    multipliers_hbm,
    out_ref,
    multipliers_ref,
    multipliers_sem,
):
    step, lifted = step_parts(received_ref, damping_ref, lifted_ref)
    multipliers = iterate_ref[...] + step * (residual_ref[...] - lifted)
    multipliers_ref[0] = multipliers
    copy = pltpu.make_async_copy(multipliers_ref, multipliers_hbm, multipliers_sem)
    copy.start()
    displaced = base_ref[0].astype(F32) - dot(recovery_ref[0], multipliers.astype(BF16))
    products = displaced * adjoint_ref[0].astype(F32)
    first = EDOF * rows_of((128, UNKNOWNS))
    lanes = lanes_of((128, UNKNOWNS))
    groups = jnp.where((lanes >= first) & (lanes < first + EDOF), 1.0, 0.0).astype(BF16)
    sums = dot(groups, jnp.concatenate(split2(products), axis=1))
    element = jnp.sum(sums, axis=1, keepdims=True) / math.sqrt(EDOF * COLS)
    voxel = voxel_ref[...]
    column = jnp.broadcast_to(voxel & 127, (128, 128)).astype(F32).T.astype(jnp.int32)
    placed = jnp.where(column == lanes_of((128, 128)), element, 0.0)
    rows = GRID_ROWS + 16
    at_row = jnp.where(rows_of((rows, 128)) - 2 == (voxel >> 7), 1.0, 0.0).astype(BF16)
    parts = dot(at_row, jnp.concatenate(split3(placed), axis=1))
    spread = parts[:, :COLS] + parts[:, COLS : 2 * COLS] + parts[:, 2 * COLS :]
    for peer in range(SUB):
        out_ref[peer] = spread[8 * peer : 8 * peer + 16]
    copy.wait()


def smooth(middle_ref, left_ref, right_ref, classes_ref, out_ref):
    beside = jnp.where(lanes_of((16, 128)) < 64, right_ref[...], left_ref[...])
    field = jnp.concatenate([middle_ref[...], beside], axis=1)
    classes = classes_ref[...]

    def moved(value, row, lane):
        if row:
            value = pltpu.roll(value, row % 16, axis=0)
        if lane:
            value = pltpu.roll(value, lane % 256, axis=1)
        return value

    for _ in range(2):
        twice = 2.0 * field
        up, down = moved(field, 1, 0), moved(field, -1, 0)
        along_rows = down + up - twice
        along_cols = moved(field, 0, -1) + moved(field, 0, 1) - twice
        diag_main = moved(down, 0, -1) + moved(up, 0, 1) - twice
        diag_anti = moved(down, 0, 1) + moved(up, 0, -1) - twice
        chosen = jnp.where(
            classes == 1.0,
            along_rows,
            jnp.where(classes == 2.0, along_cols, jnp.where(classes == 3.0, diag_main, diag_anti)),
        )
        field = field + FIBRE_RATE * chosen + ISO_RATE * (along_rows + along_cols)
        field = jnp.where(classes > 0.0, field, 0.0)
    out_ref[...] = field[2:10, :128]


def both_ways(value, axes, size, wrap):
    up = [(i, (i + 1) % size) for i in range(size if wrap else size - 1)]
    down = [(j, i) for i, j in up]
    return lax.ppermute(value, axes, up), lax.ppermute(value, axes, down)


def on_device(
    dual_ops,
    dual_rhs,
    partner,
    coarse_basis,
    coarse_inverse,
    damping,
    recovery,
    base_disp,
    adjoint,
    elem_voxel,
    fibre_class,
):
    damping = damping.reshape(1, COLS)
    tall = ((SPOTS, COLS), F32)
    to_sub = ((SUB, 16, COLS), F32)
    to_load = ((LOAD, 16, COLS), F32)
    edge = ((EDGE, COLS), BF16)
    whole = ("sub", "load")
    up = [(i, (i + 1) % (SUB * LOAD)) for i in range(SUB * LOAD)]
    down = [(j, i) for i, j in up]

    def over(value, axis):
        return lax.all_to_all(value, axis, 0, 0, tiled=True)

    sent, send, lifted = call(
        first_terms,
        [((LOAD, 64, COLS), F32), ((2 * EDGE, SPOTS), BF16), ((SPOTS, COLS), BF16)],
        (dual_rhs, coarse_basis, coarse_inverse, partner),
        "first_terms",
        scratch=[
            pltpu.VMEM(dual_rhs.shape, F32),
            pltpu.VMEM(coarse_basis.shape, BF16),
            pltpu.VMEM(coarse_inverse.shape, F32),
            pltpu.VMEM(partner.shape, jnp.int32),
            pltpu.VMEM((LOAD, 64, COLS), F32),
            pltpu.VMEM((2 * EDGE, SPOTS), BF16),
            pltpu.VMEM((SPOTS, COLS), BF16),
        ]
        + [pltpu.SemaphoreType.DMA] * 8,
        far=(0, 1, 2, 3),
        far_out=(0, 1, 2),
        limit=FIRST,
    )
    received = over(sent, "load")
    partial, block, operator = call(
        first_partial,
        [to_sub, ((COLS, 2 * SUB * 16), BF16), (dual_ops.shape, BF16)],
        (received, dual_ops),
        "first_partial",
        scratch=[pltpu.SemaphoreType.DMA] * 4,
        far=(1,),
        limit=PART,
    )
    residual = dual_rhs
    before = ()
    for iteration in range(2):
        received = over(partial, "load" if iteration else "sub")
        iterate, images, lower, upper = call(
            functools.partial(advance, iteration == 0),
            [tall, ((SPOTS, COLS), BF16), edge, edge],
            (received, damping, lifted, (operator, dual_ops)[iteration], send, residual) + before,
            "advance",
        )
        before = (iterate,)
        from_before = lax.ppermute(upper, whole, up)
        from_after = lax.ppermute(lower, whole, down)
        if iteration == 0:
            inner, pick = call(
                first_inner, [tall, ((SPOTS, SPOTS + 2 * EDGE), BF16)], (images, partner), "first_inner",
                flops=2 * SPOTS * SPOTS * 1024, moved=8 * 2**20,
            )
        else:
            inner, classes = call(
                inner_classes, [tall, ((16, 2 * COLS), F32)], (images, pick, received, middle), "inner_classes",
                flops=2 * SPOTS * SPOTS * 256, moved=4 * 2**20,
            )
        residual, sent = call(
            residual_terms,
            [tall, to_sub],
            (dual_rhs, images, inner, pick, from_before, from_after, coarse_basis, fibre_class),
            "residual_terms",
        )
        received = over(sent, "sub")
        if iteration == 0:
            partial, middle = call(
                class_partial, [to_load, ((16, COLS), F32)], (received, block, fibre_class), "class_partial"
            )
        else:
            (partial,) = call(later_partial, [to_load], (received, block), "later_partial")
    received = over(partial, "load")
    multipliers, sent = call(
        gradients,
        [((1, SPOTS, COLS), F32), to_sub],
        (received, damping, lifted, residual, iterate, recovery, base_disp, adjoint, elem_voxel),
        "gradients",
        scratch=[pltpu.VMEM((1, SPOTS, COLS), F32), pltpu.SemaphoreType.DMA],
        far_out=(0,),
    )
    middle = jnp.sum(over(sent, "sub"), axis=0)
    left, right = both_ways(middle, "load", LOAD, False)
    (field,) = call(
        smooth,
        [(fibre_class.shape, F32)],
        (middle, left, right, classes),
        "smooth",
    )
    return multipliers, field


def solution(mesh):
    placed = (
        P(("sub", "load"), None, None),
        P(("sub", "load"), None, None),
        P(("sub", "load"), None),
        P(("sub", "load"), None, None),
        P(("sub", "load"), None),
        P(),
        P(("sub", "load"), None, None),
        P(("sub", "load"), None, None),
        P(("sub", "load"), None, None),
        P(("sub", "load"), None),
        P("sub", "load"),
    )
    return jax.shard_map(
        on_device,
        mesh=mesh,
        in_specs=placed,
        out_specs=(P(("sub", "load"), None, None), P("sub", "load")),
        check_vma=False,
    )
```
